1024 devices in a mesh: gx: 8 (over x, core), gy: 32 (over z_lo, y), ha: 4 (over z_hi).
Axes of the slice: x: 4, y: 8, z: 16 (z_hi: 4, z_lo: 4; z = z_hi * 4 + z_lo), core: 2. Of those that a mesh axis runs over, the one named last changes fastest.
Arguments:
- global_state: float32 [8, 60, 64, 128], P(None, 'ha', 'gx', 'gy'), may hold values from -6 to 6
- crm_state: float32 [8, 60, 64, 8192], P(None, 'ha', 'gx', 'gy'), may hold values from -6 to 6
- mixing: float32 [8, 8], replicated, may hold values from -2 to 2
- substeps: int32 [64, 128], P('gx', 'gy'), may hold values from 1 to 8
- assignment: int32 [64, 128], P('gx', 'gy'), may hold values from 0 to 31, as said below
Outputs:
- new_global: float32 [8, 60, 64, 128], P(None, 'ha', 'gx', 'gy')
- new_crm: float32 [8, 60, 524288], P(None, None, ('gx', 'gy', 'ha'))
The draws below stay inside these ranges and needn't reach their ends.
Inputs may be any that keep to these rules, and one draw needn't show every extreme that they name: `assignment`: within each tile of 8 x 4 columns every value 0 .. 31 appears once; value // 8 is the helper index, value % 8 the slot on that helper.
All inputs are finite; a program needn't handle non-finite values.
Results may differ from the reference program's by a relative error of at most 0.0003.
Values sent between devices are 32-bit elements; how exact they have to be, the bound alone decides.
No kernel may reach another device: no remote copies, remote signals or barrier semaphores. Data moves between devices by JAX's collectives and lax.ppermute only.
A program may use at most 64 MiB of HBM per device.

```python
import jax
import jax.numpy as jnp
from jax import lax

CX = 8
CY = 4
GF = 8
CF = 8
LEV = 60
CC = 64
MAXSUB = 8
GSUB = 4
NXG = 64
NYG = 128
SLOTS = 8
N_GX = 8
N_GY = 32


def joint_draw(key):
    base = jax.random.fold_in(key, 31)
    counts = jax.random.randint(jax.random.fold_in(base, 1), (NXG, NYG), 1, 9)
    tiles_x = NXG // CX
    tiles_y = NYG // CY
    columns = CX * CY
    helpers = columns // SLOTS
    tiled = counts.reshape(tiles_x, CX, tiles_y, CY).transpose(0, 2, 1, 3).reshape(tiles_x * tiles_y, columns)
    noise = jax.random.randint(jax.random.fold_in(base, 2), tiled.shape, 0, 64)
    score = (tiled * 64 + noise) * columns + jnp.arange(columns, dtype=jnp.int32)[None, :]
    order = jnp.argsort(-score, axis=1, stable=True)
    ranking = jnp.argsort(order, axis=1, stable=True)
    lanes = ranking % helpers
    rounds = ranking // helpers
    helper = jnp.where(rounds % 2 == 0, lanes, helpers - 1 - lanes)
    values = helper * SLOTS + rounds
    placed = values.reshape(tiles_x, tiles_y, CX, CY).transpose(0, 2, 1, 3).reshape(NXG, NYG)
    return (counts.astype(jnp.int32), placed.astype(jnp.int32))


def draw_substeps(key, part):
    return joint_draw(key)[0]


def draw_assignment(key, part):
    return joint_draw(key)[1]


def steps_of(key, dims, shards, smallest, largest):
    gain = 1.0
    for position, blocks in shards:
        steps = jax.random.uniform(jax.random.fold_in(jax.random.fold_in(key, 6), position), (blocks,), jnp.float32, smallest / len(shards), largest / len(shards))
        gain = gain * jnp.repeat(jnp.exp(steps), dims[position] // blocks).reshape((-1,) + (1,) * (len(dims) - 1 - position))
    return gain


def gaussian(own_key, extent, width, most, shards=(), held_as=jnp.bfloat16):
    drawn = jax.random.normal(own_key, extent, jnp.float32) * width
    if len(shards) > 0:
        drawn = steps_of(own_key, extent, shards, -0.22, 0.18) * drawn
    return jnp.clip(drawn, min=-most, max=most).astype(held_as)


def setup_inputs(seed: int = 0) -> dict:
    seeds = jax.random.split(jax.random.key(seed), 6)
    global_state = gaussian(seeds[0], (GF, LEV, NXG, NYG), 1.0, 6.0, ((1, 4), (2, 8), (3, 32)), jnp.float32)
    crm_state = gaussian(seeds[1], (CF, LEV, NXG, NYG * CC), 1.0, 6.0, ((1, 4), (2, 8), (3, 32)), jnp.float32)
    mixing = gaussian(seeds[2], (CF, CF), CF ** -0.5, 2.0, (), jnp.float32)
    substeps = draw_substeps(jax.random.fold_in(seeds[5], 71), 0)
    assignment = draw_assignment(jax.random.fold_in(seeds[5], 71), 0)
    return dict(global_state=global_state, crm_state=crm_state, mixing=mixing, substeps=substeps, assignment=assignment)


HIGH = lax.Precision.HIGHEST


def global_operator(field):
    east = jnp.roll(field, -1, axis=2)
    west = jnp.roll(field, 1, axis=2)
    north = jnp.roll(field, -1, axis=3)
    south = jnp.roll(field, 1, axis=3)
    return 0.2 * (east + west + north + south - 4.0 * field) - 0.15 * (east - west) - 0.15 * (north - south)


def crm_update(state, pushed, mixing):
    lateral = jnp.roll(state, 1, axis=3) + jnp.roll(state, -1, axis=3) - 2.0 * state
    upper = jnp.concatenate([state[:, :1], state[:, :-1]], axis=1)
    lower = jnp.concatenate([state[:, 1:], state[:, -1:]], axis=1)
    coupling = jnp.einsum('gf,flsc->glsc', mixing, jnp.tanh(state), precision=HIGH)
    return state + 0.1 * (1.0 * lateral + 0.5 * (upper + lower - 2.0 * state) + pushed + coupling)


def to_tiles(array, lead):
    shaped = array.reshape(array.shape[:lead] + (N_GX, CX, N_GY, CY))
    moved = jnp.moveaxis(shaped, (lead, lead + 2), (0, 1))
    return moved.reshape((N_GX * N_GY,) + array.shape[:lead] + (CX * CY,))


def from_tiles(array, lead):
    inner = array.shape[1:1 + lead]
    shaped = array.reshape((N_GX, N_GY) + inner + (CX, CY))
    moved = jnp.moveaxis(shaped, (0, 1), (lead, lead + 2))
    return moved.reshape(inner + (CX * N_GX, CY * N_GY))


def reference(global_state, crm_state, mixing, substeps, assignment):
    current = global_state
    for substep in range(GSUB):
        current = current + 0.5 * global_operator(current)
    forcing = (current - global_state) / (0.5 * GSUB)
    columns = CX * CY
    shaped = crm_state.reshape(CF, LEV, N_GX, CX, N_GY, CY, CC)
    shaped = jnp.moveaxis(shaped, (2, 4), (0, 1))
    state_tiles = shaped.reshape(N_GX * N_GY, CF, LEV, columns, CC)
    forcing_tiles = to_tiles(forcing, 2)
    count_tiles = to_tiles(substeps, 0)
    assign_tiles = to_tiles(assignment, 0)

    def per_tile(inputs):
        states, pushes, counts, assigned = inputs
        onehot = (assigned[:, None] == jnp.arange(columns, dtype=jnp.int32)[None, :]).astype(jnp.float32)
        slotted = jnp.einsum('flxc,xj->fljc', states, onehot, precision=HIGH)
        pushed = jnp.einsum('glx,xj->glj', pushes, onehot, precision=HIGH)[:, :, :, None]
        slot_counts = jnp.dot(counts.astype(jnp.float32), onehot, precision=HIGH).astype(jnp.int32)

        def one_step(index, state):
            updated = crm_update(state, pushed, mixing)
            return jnp.where((index < slot_counts)[:, None], updated, state)

        final = lax.fori_loop(0, MAXSUB, one_step, slotted)
        tendency = jnp.mean(final - slotted, axis=3)
        placed = jnp.einsum('flj,xj->flx', tendency, onehot, precision=HIGH)
        return final, placed

    finals, placed = lax.map(per_tile, (state_tiles, forcing_tiles, count_tiles, assign_tiles))
    new_crm = jnp.moveaxis(finals, 0, 2).reshape((CF, LEV, N_GX * N_GY * columns * CC))
    new_global = current + from_tiles(placed, 2)
    return new_global, new_crm
```

```python
import jax
import jax.numpy as jnp
from jax import lax
from jax.experimental import pallas as pl
from jax.experimental.pallas import tpu as pltpu
from jax.sharding import PartitionSpec as P

MAXSUB = 8
GSUB = 4
HIGH = lax.Precision.HIGHEST
FIELDS = 8
PART = 15
ROWS = FIELDS * PART
PITCH = 16
LANES = 128
WIDTH = 64
TX = 8
TY = 4
COLS = TX * TY
HELP = 4
SLOTS = 8
PAIRS = SLOTS // 2
LEVELS = PART * HELP
BASE = 8
SROWS = 80
BLOCKS = 8

VM = pltpu.CompilerParams(vmem_limit_bytes=32 * 1024 * 1024)


def smem():
    return pl.BlockSpec(memory_space=pltpu.SMEM)


def vmem():
    return pl.BlockSpec(memory_space=pltpu.VMEM)


def slotting_kernel(assign_ref, crm_ref, out_ref, inverse, held, sems):
    loads = [
        pltpu.make_async_copy(crm_ref.at[:, i * LANES : (i + 1) * LANES], held.at[i], sems.at[i]) for i in range(TY // 2)
    ]
    for load in loads:
        load.start()
    for x in range(TX):
        for y in range(TY):
            inverse[assign_ref[y, x]] = x * TY + y
    lane = lax.broadcasted_iota(jnp.int32, (ROWS, LANES), 1)

    def column(slot, half):
        place = inverse[slot]
        x = place // TY
        y = place % TY
        rows = held[y // 2, pl.ds(x, ROWS, stride=TX), :]
        return pltpu.roll(rows, ((y % 2) ^ half) * WIDTH, 1)

    for load in loads:
        load.wait()
    for helper in range(HELP):
        for pair in range(PAIRS):
            slot = helper * SLOTS + 2 * pair
            out_ref[helper, pair * ROWS : (pair + 1) * ROWS, :] = jnp.where(
                lane < WIDTH, column(slot, 0), column(slot + 1, 1)
            )


def forcing_kernel(assign_ref, own_ref, south_ref, north_ref, west_ref, east_ref, g4_ref, f0_ref, f1_ref, f2_ref, f3_ref, ext, cols):
    me = lax.axis_index("ha")
    ext[:, 0:4, :] = west_ref[...]
    ext[0:4, 4:12, :] = south_ref[...]
    ext[4:8, 4:12, :] = own_ref[...]
    ext[8:12, 4:12, :] = north_ref[...]
    ext[:, 12:16, :] = east_ref[...]
    g = ext[...]
    for _ in range(GSUB):
        center = g[1:-1]
        east = jnp.stack([pltpu.roll(center[i], 15, 0) for i in range(center.shape[0])])
        west = jnp.stack([pltpu.roll(center[i], 1, 0) for i in range(center.shape[0])])
        north = g[2:]
        south = g[:-2]
        step = 0.2 * (east + west + north + south - 4.0 * center) - 0.15 * (east - west) - 0.15 * (north - south)
        g = center + 0.5 * step
    for y in range(TY):
        last = pltpu.roll(g[y], 12, 0)[:TX]
        g4_ref[y] = last
        cols[y] = (last - own_ref[y]) / (0.5 * GSUB)
    parts = (f0_ref, f1_ref, f2_ref, f3_ref)
    for x in range(TX):
        for y in range(TY):
            slot = assign_ref[y, x]
            away = (slot // SLOTS - me) & (HELP - 1)
            row = slot & (SLOTS - 1)
            for k in range(HELP):

                @pl.when(away == k)
                def _():
                    parts[k][pl.ds(row, 1), :] = cols[y, x : x + 1, :]


def advance_kernel(
    assign_ref, sub_ref, mix_ref, r_ref, f0_ref, f1_ref, f2_ref, f3_ref, out_ref, tend_ref, counts, one, two, push, gather, weights
):
    pair = pl.program_id(0)
    me = lax.axis_index("ha")

    @pl.when(pair == 0)
    def _():
        for x in range(TX):
            for y in range(TY):
                counts[assign_ref[y, x]] = sub_ref[y, x]
        tend_ref[...] = jnp.zeros_like(tend_ref)
        gather[...] = jnp.zeros_like(gather)
        for h in range(FIELDS):
            for g in range(FIELDS):
                weights[h, g] = jnp.full((8, LANES), 0.1 * mix_ref[h, g], jnp.float32)

    first = me * SLOTS + 2 * pair
    n0 = counts[first]
    n1 = counts[first + 1]
    lane8 = lax.broadcasted_iota(jnp.int32, (8, LANES), 1)
    limit = jnp.where(lane8 < WIDTH, n0, n1)
    steps = jnp.maximum(n0, n1)

    slot_row = lax.broadcasted_iota(jnp.int32, (SLOTS, LANES), 0)
    slot_lane = lax.broadcasted_iota(jnp.int32, (SLOTS, LANES), 1)
    chosen = slot_row == 2 * pair + slot_lane // WIDTH
    spread = jnp.where(chosen, 0.1, 0.0).astype(jnp.float32)
    averaging = jnp.where(chosen, 1.0 / WIDTH, 0.0).astype(jnp.float32)
    parts = (f0_ref, f1_ref, f2_ref, f3_ref)
    for away in range(HELP):
        start = ((me - away) & (HELP - 1)) * PART
        wide = lax.dot_general(
            parts[away][...], spread, (((0,), (0,)), ((), ())), precision=HIGH, preferred_element_type=jnp.float32
        )
        for f in range(FIELDS):
            push[f, pl.ds(start, PART), :] = wide[f * PITCH : f * PITCH + PART]

    def ends(ref):
        for f in range(FIELDS):
            ref[f, BASE - 1 : BASE, :] = ref[f, BASE : BASE + 1, :]
            ref[f, BASE + LEVELS : BASE + LEVELS + 1, :] = ref[f, BASE + LEVELS - 1 : BASE + LEVELS, :]

    for k in range(HELP):
        for f in range(FIELDS):
            one[f, BASE + k * PART : BASE + (k + 1) * PART, :] = r_ref[k, f * PART : (f + 1) * PART, :]
    ends(one)

    inner = lane8 & (WIDTH - 1)
    last = inner == WIDTH - 1
    zeroth = inner == 0

    def substep(source, target, index):
        active = index < limit
        for b in range(BLOCKS):
            row = BASE + 8 * b
            here = [source[f, row : row + 8, :] for f in range(FIELDS)]
            warm = [jnp.tanh(s) for s in here]
            for h in range(FIELDS):
                s = here[h]
                other = pltpu.roll(s, WIDTH, 1)
                right = pltpu.roll(jnp.where(zeroth, other, s), LANES - 1, 1)
                left = pltpu.roll(jnp.where(last, other, s), 1, 1)
                upper = source[h, row - 1 : row + 7, :]
                lower = source[h, row + 1 : row + 9, :]
                mixed = weights[h, 0] * warm[0]
                for g in range(1, FIELDS):
                    mixed = mixed + weights[h, g] * warm[g]
                total = 0.7 * s + push[h, 8 * b : 8 * b + 8, :]
                total = total + 0.1 * (right + left) + 0.05 * (upper + lower)
                target[h, row : row + 8, :] = jnp.where(active, total + mixed, s)
        ends(target)

    def both(index, _):
        substep(one, two, 2 * index)
        substep(two, one, 2 * index + 1)
        return 0

    lax.fori_loop(0, (steps + 1) // 2, both, 0)

    for f in range(FIELDS):
        for b in range(BLOCKS):
            n = min(8, LEVELS - 8 * b)
            out_ref[pl.ds(8 * b * FIELDS + f, n, stride=FIELDS), :] = one[f, BASE + 8 * b : BASE + 8 * b + n, :]
    for k in range(HELP):
        for f in range(FIELDS):
            gather[f * PITCH : f * PITCH + PART, :] = (
                one[f, BASE + k * PART : BASE + (k + 1) * PART, :] - r_ref[k, f * PART : (f + 1) * PART, :]
            )
        tend_ref[k] += lax.dot_general(
            averaging, gather[...], (((1,), (1,)), ((), ())), precision=HIGH, preferred_element_type=jnp.float32
        )


def placing_kernel(assign_ref, g4_ref, tend_ref, out_ref):
    for x in range(TX):
        for y in range(TY):
            out_ref[y, x : x + 1, :] = g4_ref[y, x : x + 1, :] + tend_ref[pl.ds(assign_ref[y, x], 1), :]


def shifted(count, by):
    return [(i, (i + by) % count) for i in range(count)]


def on_device(global_state, crm_state, mixing, substeps, assignment):
    f32 = jnp.float32
    assignment = assignment.T
    substeps = substeps.T
    own = jnp.pad(global_state, ((0, 0), (0, PITCH - PART), (0, 0), (0, 0)))
    own = own.transpose(3, 2, 0, 1).reshape(TY, TX, LANES)
    ny = lax.axis_size("gy")
    nx = lax.axis_size("gx")
    south = lax.ppermute(own, "gy", shifted(ny, 1))
    north = lax.ppermute(own, "gy", shifted(ny, -1))

    slotted = pl.pallas_call(
        slotting_kernel,
        out_shape=jax.ShapeDtypeStruct((HELP, PAIRS * ROWS, LANES), f32),
        in_specs=[smem(), pl.BlockSpec(memory_space=pl.ANY)],
        out_specs=vmem(),
        scratch_shapes=[
            pltpu.SMEM((COLS,), jnp.int32),
            pltpu.VMEM((TY // 2, ROWS * TX, LANES), f32),
            pltpu.SemaphoreType.DMA((TY // 2,)),
        ],
        compiler_params=VM,
    )(assignment, crm_state.reshape(ROWS * TX, TY * WIDTH))
    slotted, south, north = lax.optimization_barrier((slotted, south, north))
    arrived = lax.all_to_all(slotted, "ha", split_axis=0, concat_axis=0, tiled=True)

    tall = jnp.concatenate([south, own, north], axis=0)
    west = lax.ppermute(tall[:, TX - 4 :], "gx", shifted(nx, 1))
    east = lax.ppermute(tall[:, :4], "gx", shifted(nx, -1))
    rowshape = jax.ShapeDtypeStruct((SLOTS, LANES), f32)
    g4, f0, f1, f2, f3 = pl.pallas_call(
        forcing_kernel,
        out_shape=[jax.ShapeDtypeStruct((TY, TX, LANES), f32)] + [rowshape] * HELP,
        in_specs=[smem()] + [vmem()] * 5,
        out_specs=[vmem()] * 5,
        scratch_shapes=[pltpu.VMEM((12, 16, LANES), f32), pltpu.VMEM((TY, TX, LANES), f32)],
        compiler_params=VM,
    )(assignment, own, south, north, west, east)
    pushes = [f0] + [
        lax.ppermute(part, "ha", shifted(HELP, away)) for away, part in ((1, f1), (2, f2), (3, f3))
    ]

    whole = pl.BlockSpec((SLOTS, LANES), lambda p: (0, 0))
    final, tendency = pl.pallas_call(
        advance_kernel,
        grid=(PAIRS,),
        out_shape=[
            jax.ShapeDtypeStruct((LEVELS * FIELDS, SLOTS * WIDTH), f32),
            jax.ShapeDtypeStruct((HELP, SLOTS, LANES), f32),
        ],
        in_specs=[smem(), smem(), smem(), pl.BlockSpec((HELP, ROWS, LANES), lambda p: (0, p, 0))] + [whole] * HELP,
        out_specs=[
            pl.BlockSpec((LEVELS * FIELDS, LANES), lambda p: (0, p)),
            pl.BlockSpec((HELP, SLOTS, LANES), lambda p: (0, 0, 0)),
        ],
        scratch_shapes=[
            pltpu.SMEM((COLS,), jnp.int32),
            pltpu.VMEM((FIELDS, SROWS, LANES), f32),
            pltpu.VMEM((FIELDS, SROWS, LANES), f32),
            pltpu.VMEM((FIELDS, 64, LANES), f32),
            pltpu.VMEM((FIELDS * PITCH, LANES), f32),
            pltpu.VMEM((FIELDS, FIELDS, 8, LANES), f32),
        ],
        compiler_params=VM,
    )(assignment, substeps, mixing, arrived, *pushes)
    returned = lax.all_to_all(tendency, "ha", split_axis=0, concat_axis=0, tiled=True)
    placed = pl.pallas_call(
        placing_kernel,
        out_shape=jax.ShapeDtypeStruct((TY, TX, LANES), f32),
        in_specs=[smem(), vmem(), vmem()],
        out_specs=vmem(),
        compiler_params=VM,
    )(assignment, g4, returned.reshape(COLS, LANES))
    new_global = placed.reshape(TY, TX, FIELDS, PITCH)[..., :PART].transpose(2, 3, 1, 0)
    new_crm = final.reshape(LEVELS, FIELDS, SLOTS * WIDTH).transpose(1, 0, 2)
    return new_global, new_crm


def solution(mesh):
    in_specs = (
        P(None, "ha", "gx", "gy"),
        P(None, "ha", "gx", "gy"),
        P(),
        P("gx", "gy"),
        P("gx", "gy"),
    )
    out_specs = (P(None, "ha", "gx", "gy"), P(None, None, ("gx", "gy", "ha")))
    return jax.shard_map(
        on_device, mesh=mesh, in_specs=in_specs, out_specs=out_specs, check_vma=False
    )
```

```python
import jax
import jax.numpy as jnp
from jax import lax
from jax.experimental import pallas as pl
from jax.experimental.pallas import tpu as pltpu
from jax.sharding import PartitionSpec as P

MAXSUB = 8
GSUB = 4
FIELDS = 8
PART = 15
ROWS = FIELDS * PART
PITCH = 16
LANES = 128
WIDTH = 64
TX = 8
TY = 4
COLS = TX * TY
HELP = 4
SLOTS = 8
PAIRS = SLOTS // 2
LEVELS = PART * HELP
BASE = 8
SROWS = 80
BLOCKS = 8
PIECES = (0, PART - 8)

VM = pltpu.CompilerParams(vmem_limit_bytes=32 * 1024 * 1024)


def smem():
    return pl.BlockSpec(memory_space=pltpu.SMEM)


def vmem():
    return pl.BlockSpec(memory_space=pltpu.VMEM)


def slotting_kernel(assign_ref, crm_ref, out_ref, inverse, held, sems):
    loads = [
        pltpu.make_async_copy(crm_ref.at[:, i * LANES : (i + 1) * LANES], held.at[i], sems.at[i]) for i in range(TY // 2)
    ]
    for load in loads:
        load.start()
    for x in range(TX):
        for y in range(TY):
            inverse[assign_ref[y, x]] = x * TY + y
    lane = lax.broadcasted_iota(jnp.int32, (ROWS, LANES), 1)

    def column(slot, half):
        place = inverse[slot]
        x = place // TY
        y = place % TY
        rows = held[y // 2, pl.ds(x, ROWS, stride=TX), :]
        return pltpu.roll(rows, ((y % 2) ^ half) * WIDTH, 1)

    for load in loads:
        load.wait()
    for helper in range(HELP):
        for pair in range(PAIRS):
            slot = helper * SLOTS + 2 * pair
            out_ref[helper, pair * ROWS : (pair + 1) * ROWS, :] = jnp.where(
                lane < WIDTH, column(slot, 0), column(slot + 1, 1)
            )


def forcing_kernel(assign_ref, own_ref, south_ref, north_ref, west_ref, east_ref, g4_ref, f0_ref, f1_ref, f2_ref, f3_ref, ext, rows):
    me = lax.axis_index("ha")
    ext[:, 0:4, :] = west_ref[...]
    ext[0:4, 4:12, :] = south_ref[...]
    ext[4:8, 4:12, :] = own_ref[...]
    ext[8:12, 4:12, :] = north_ref[...]
    ext[:, 12:16, :] = east_ref[...]
    g = ext[...]
    for _ in range(GSUB):
        center = g[1:-1]
        east = jnp.stack([pltpu.roll(center[i], 15, 0) for i in range(center.shape[0])])
        west = jnp.stack([pltpu.roll(center[i], 1, 0) for i in range(center.shape[0])])
        north = g[2:]
        south = g[:-2]
        step = 0.2 * (east + west + north + south - 4.0 * center) - 0.15 * (east - west) - 0.15 * (north - south)
        g = center + 0.5 * step
    for y in range(TY):
        last = pltpu.roll(g[y], 12, 0)[:TX]
        g4_ref[y] = last
        forcing = (last - own_ref[y]) / (0.5 * GSUB)
        for x in range(TX):
            slot = assign_ref[y, x]
            rows[slot // SLOTS, pl.ds(slot & (SLOTS - 1), 1), :] = forcing[x : x + 1]
    for k, part in enumerate((f0_ref, f1_ref, f2_ref, f3_ref)):
        part[...] = rows[me ^ k]


def split(value):
    high = value.astype(jnp.bfloat16)
    rest = value - high.astype(jnp.float32)
    middle = rest.astype(jnp.bfloat16)
    low = (rest - middle.astype(jnp.float32)).astype(jnp.bfloat16)
    return high, middle, low


def advance_kernel(
    assign_ref,
    sub_ref,
    mix_ref,
    r_ref,
    f0_ref,
    f1_ref,
    f2_ref,
    f3_ref,
    out_ref,
    tend_ref,
    counts,
    one,
    two,
    push,
    gather,
    held,
    weights,
    staged,
    sems,
):
    me = lax.axis_index("ha")
    for x in range(TX):
        for y in range(TY):
            counts[assign_ref[y, x]] = sub_ref[y, x]
    tend_ref[...] = jnp.zeros_like(tend_ref)
    gather[...] = jnp.zeros_like(gather)
    for h in range(FIELDS):
        for g in range(FIELDS):
            weights[h, g] = jnp.full((8, LANES), 0.1 * mix_ref[h, g], jnp.float32)
    lane8 = lax.broadcasted_iota(jnp.int32, (8, LANES), 1)
    half = lane8 & WIDTH
    to_right = half | ((lane8 + 1) & (WIDTH - 1))
    to_left = half | ((lane8 + WIDTH - 1) & (WIDTH - 1))
    slot_row = lax.broadcasted_iota(jnp.int32, (SLOTS, LANES), 0)
    slot_pair = lax.broadcasted_iota(jnp.int32, (SLOTS, LANES), 1) // WIDTH
    forcings = (f0_ref, f1_ref, f2_ref, f3_ref)

    def ends(ref):
        for f in range(FIELDS):
            ref[f, BASE - 1 : BASE, :] = ref[f, BASE : BASE + 1, :]
            ref[f, BASE + LEVELS : BASE + LEVELS + 1, :] = ref[f, BASE + LEVELS - 1 : BASE + LEVELS, :]

    def send(pair, buffer):
        return pltpu.make_async_copy(
            staged.at[buffer], out_ref.at[:, pl.ds(pl.multiple_of(pair * LANES, LANES), LANES)], sems.at[buffer]
        )

    def one_pair(pair, buffer):
        first = me * SLOTS + 2 * pair
        n0 = counts[first]
        n1 = counts[first + 1]
        limit = jnp.where(lane8 < WIDTH, n0, n1)
        steps = jnp.maximum(n0, n1)
        chosen = slot_row == 2 * pair + slot_pair
        spread = jnp.where(chosen, 1.0, 0.0).astype(jnp.bfloat16)
        averaging = jnp.where(chosen, 1.0 / WIDTH, 0.0).astype(jnp.bfloat16)

        for k in range(HELP):
            terms = split(0.1 * forcings[k][...])
            total = None
            for term in terms:
                part = lax.dot_general(term, spread, (((0,), (0,)), ((), ())), preferred_element_type=jnp.float32)
                total = part if total is None else total + part
            held[k] = total
            start = (me ^ k) * PART
            for f in range(FIELDS):
                for i in PIECES:
                    push[f, pl.ds(start + i, 8), :] = held[k, f * PITCH + i : f * PITCH + i + 8, :]
        for k in range(HELP):
            for f in range(FIELDS):
                for i in PIECES:
                    row = BASE + k * PART + i
                    one[f, row : row + 8, :] = r_ref[k, pl.ds(pair * ROWS + f * PART + i, 8), :]
        ends(one)

        def substep(source, target, index):
            active = index < limit
            for b in range(BLOCKS):
                row = BASE + 8 * b
                here = [source[f, row : row + 8, :] for f in range(FIELDS)]
                warm = [jnp.tanh(s) for s in here]
                for h in range(FIELDS):
                    s = here[h]
                    right = jnp.take_along_axis(s, to_right, axis=1)
                    left = jnp.take_along_axis(s, to_left, axis=1)
                    upper = source[h, row - 1 : row + 7, :]
                    lower = source[h, row + 1 : row + 9, :]
                    mixed = weights[h, 0] * warm[0]
                    for g in range(1, FIELDS):
                        mixed = mixed + weights[h, g] * warm[g]
                    total = 0.7 * s + push[h, 8 * b : 8 * b + 8, :]
                    total = total + 0.1 * (right + left) + 0.05 * (upper + lower)
                    target[h, row : row + 8, :] = jnp.where(active, total + mixed, s)
            ends(target)

        def twice(index, _):
            substep(one, two, 2 * index)
            substep(two, one, 2 * index + 1)
            return 0

        lax.fori_loop(0, (steps + 1) // 2, twice, 0)

        for f in range(FIELDS):
            for b in range(BLOCKS):
                n = min(8, LEVELS - 8 * b)
                staged[buffer, pl.ds(8 * b * FIELDS + f, n, stride=FIELDS), :] = one[f, BASE + 8 * b : BASE + 8 * b + n, :]
        send(pair, buffer).start()
        for k in range(HELP):
            for f in range(FIELDS):
                for i in PIECES:
                    row = BASE + k * PART + i
                    gather[f * PITCH + i : f * PITCH + i + 8, :] = (
                        one[f, row : row + 8, :] - r_ref[k, pl.ds(pair * ROWS + f * PART + i, 8), :]
                    )
            for term in split(gather[...]):
                tend_ref[k] += lax.dot_general(
                    averaging, term, (((1,), (1,)), ((), ())), preferred_element_type=jnp.float32
                )

    def each(pair, _):
        one_pair(pair, pair)
        return 0

    lax.fori_loop(0, PAIRS, each, 0)
    for pair in range(PAIRS):
        send(pair, pair).wait()


def placing_kernel(assign_ref, g4_ref, tend_ref, out_ref):
    for x in range(TX):
        for y in range(TY):
            out_ref[y, x : x + 1, :] = g4_ref[y, x : x + 1, :] + tend_ref[pl.ds(assign_ref[y, x], 1), :]


def swaps(count, first):
    pairs = [(i, (i + 1) % count) for i in range(first, count, 2)]
    return pairs + [(b, a) for a, b in pairs]


def on_device(global_state, crm_state, mixing, substeps, assignment):
    f32 = jnp.float32
    assignment = assignment.T
    substeps = substeps.T
    own = jnp.pad(global_state, ((0, 0), (0, PITCH - PART), (0, 0), (0, 0)))
    own = own.transpose(3, 2, 0, 1).reshape(TY, TX, LANES)
    ny = lax.axis_size("gy")
    nx = lax.axis_size("gx")
    odd = lax.axis_index("gy") % 2 == 1
    outer = lax.ppermute(own, "gy", swaps(ny, 1))
    inner = lax.ppermute(own, "gy", swaps(ny, 0))

    slotted = pl.pallas_call(
        slotting_kernel,
        out_shape=jax.ShapeDtypeStruct((HELP, PAIRS * ROWS, LANES), f32),
        in_specs=[smem(), pl.BlockSpec(memory_space=pltpu.HBM)],
        out_specs=vmem(),
        scratch_shapes=[
            pltpu.SMEM((COLS,), jnp.int32),
            pltpu.VMEM((TY // 2, ROWS * TX, LANES), f32),
            pltpu.SemaphoreType.DMA((TY // 2,)),
        ],
        compiler_params=pltpu.CompilerParams(vmem_limit_bytes=60 * 1024 * 1024),
    )(assignment, crm_state.reshape(ROWS * TX, TY * WIDTH))
    slotted, outer, inner = lax.optimization_barrier((slotted, outer, inner))
    arrived = lax.all_to_all(slotted, "ha", split_axis=0, concat_axis=0, tiled=True)

    south = jnp.where(odd, inner, outer)
    north = jnp.where(odd, outer, inner)
    tall = jnp.concatenate([south, own, north], axis=0)
    odd = lax.axis_index("gx") % 2 == 1
    low, high = tall[:, :4], tall[:, TX - 4 :]
    outer = lax.ppermute(jnp.where(odd, high, low), "gx", swaps(nx, 1))
    inner = lax.ppermute(jnp.where(odd, low, high), "gx", swaps(nx, 0))
    west = jnp.where(odd, inner, outer)
    east = jnp.where(odd, outer, inner)
    rowshape = jax.ShapeDtypeStruct((SLOTS, LANES), f32)
    g4, *pushes = pl.pallas_call(
        forcing_kernel,
        out_shape=[jax.ShapeDtypeStruct((TY, TX, LANES), f32)] + [rowshape] * HELP,
        in_specs=[smem()] + [vmem()] * 5,
        out_specs=[vmem()] * 5,
        scratch_shapes=[pltpu.VMEM((12, 16, LANES), f32), pltpu.VMEM((HELP, SLOTS, LANES), f32)],
        compiler_params=VM,
    )(assignment, own, south, north, west, east)
    for k in range(1, HELP):
        pushes[k] = lax.ppermute(pushes[k], "ha", [(i, i ^ k) for i in range(HELP)])

    final, tendency = pl.pallas_call(
        advance_kernel,
        out_shape=[
            jax.ShapeDtypeStruct((LEVELS * FIELDS, SLOTS * WIDTH), f32),
            jax.ShapeDtypeStruct((HELP, SLOTS, LANES), f32),
        ],
        in_specs=[smem(), smem(), smem()] + [vmem()] * (1 + HELP),
        out_specs=[pl.BlockSpec(memory_space=pltpu.HBM), vmem()],
        scratch_shapes=[
            pltpu.SMEM((COLS,), jnp.int32),
            pltpu.VMEM((FIELDS, SROWS, LANES), f32),
            pltpu.VMEM((FIELDS, SROWS, LANES), f32),
            pltpu.VMEM((FIELDS, 64, LANES), f32),
            pltpu.VMEM((FIELDS * PITCH, LANES), f32),
            pltpu.VMEM((HELP, FIELDS * PITCH, LANES), f32),
            pltpu.VMEM((FIELDS, FIELDS, 8, LANES), f32),
            pltpu.VMEM((PAIRS, LEVELS * FIELDS, LANES), f32),
            pltpu.SemaphoreType.DMA((PAIRS,)),
        ],
        compiler_params=VM,
    )(assignment, substeps, mixing, arrived, *pushes)
    returned = lax.all_to_all(tendency, "ha", split_axis=0, concat_axis=0, tiled=True)
    placed = pl.pallas_call(
        placing_kernel,
        out_shape=jax.ShapeDtypeStruct((TY, TX, LANES), f32),
        in_specs=[smem(), vmem(), vmem()],
        out_specs=vmem(),
        compiler_params=VM,
    )(assignment, g4, returned.reshape(COLS, LANES))
    new_global = placed.reshape(TY, TX, FIELDS, PITCH)[..., :PART].transpose(2, 3, 1, 0)
    new_crm = final.reshape(LEVELS, FIELDS, SLOTS * WIDTH).transpose(1, 0, 2)
    return new_global, new_crm


def solution(mesh):
    in_specs = (
        P(None, "ha", "gx", "gy"),
        P(None, "ha", "gx", "gy"),
        P(),
        P("gx", "gy"),
        P("gx", "gy"),
    )
    out_specs = (P(None, "ha", "gx", "gy"), P(None, None, ("gx", "gy", "ha")))
    return jax.shard_map(
        on_device, mesh=mesh, in_specs=in_specs, out_specs=out_specs, check_vma=False
    )
```

```python
import jax
import jax.numpy as jnp
from jax import lax
from jax.experimental import pallas as pl
from jax.experimental.pallas import tpu as pltpu
from jax.sharding import PartitionSpec as P

MAXSUB = 8
GSUB = 4
FIELDS = 8
PART = 15
ROWS = FIELDS * PART
PITCH = 16
LANES = 128
WIDTH = 64
TX = 8
TY = 4
COLS = TX * TY
HELP = 4
ORDER = (0, 1, 3, 2)
SLOTS = 8
PAIRS = SLOTS // 2
LEVELS = PART * HELP
BASE = 8
SROWS = 80
BLOCKS = 8
PIECES = (0, PART - 8)

VM = pltpu.CompilerParams(vmem_limit_bytes=32 * 1024 * 1024)


def smem():
    return pl.BlockSpec(memory_space=pltpu.SMEM)


def vmem():
    return pl.BlockSpec(memory_space=pltpu.VMEM)


def slotting_kernel(assign_ref, crm_ref, s0_ref, s1_ref, s2_ref, s3_ref, inverse, held, sems):
    me = lax.axis_index("ha")
    loads = [
        pltpu.make_async_copy(crm_ref.at[:, i * LANES : (i + 1) * LANES], held.at[i], sems.at[i]) for i in range(TY // 2)
    ]
    for load in loads:
        load.start()
    for x in range(TX):
        for y in range(TY):
            inverse[assign_ref[y, x]] = x * TY + y
    lane = lax.broadcasted_iota(jnp.int32, (ROWS, LANES), 1)

    def column(slot, half):
        place = inverse[slot]
        x = place // TY
        y = place % TY
        rows = held[y // 2, pl.ds(x, ROWS, stride=TX), :]
        return pltpu.roll(rows, ((y % 2) ^ half) * WIDTH, 1)

    for load in loads:
        load.wait()
    for k, part in enumerate((s0_ref, s1_ref, s2_ref, s3_ref)):
        for pair in range(PAIRS):
            slot = (me ^ ORDER[k]) * SLOTS + 2 * pair
            part[pair * ROWS : (pair + 1) * ROWS, :] = jnp.where(lane < WIDTH, column(slot, 0), column(slot + 1, 1))


def choose(odd, first, second):
    return jnp.where(odd, first, second)


def border_kernel(own_ref, outer_ref, inner_ref, to_outer_ref, to_inner_ref, tall):
    odd = lax.axis_index("gy") % 2 == 1
    tall[0:4] = choose(odd, inner_ref[...], outer_ref[...])
    tall[4:8] = own_ref[...]
    tall[8:12] = choose(odd, outer_ref[...], inner_ref[...])
    odd = lax.axis_index("gx") % 2 == 1
    low, high = tall[:, 0:4, :], tall[:, TX - 4 : TX, :]
    to_outer_ref[...] = choose(odd, high, low)
    to_inner_ref[...] = choose(odd, low, high)


def forcing_kernel(assign_ref, own_ref, outery_ref, innery_ref, outerx_ref, innerx_ref, g4_ref, f0_ref, f1_ref, f2_ref, f3_ref, ext, rows):
    me = lax.axis_index("ha")
    odd = lax.axis_index("gy") % 2 == 1
    ext[0:4, 4:12, :] = choose(odd, innery_ref[...], outery_ref[...])
    ext[4:8, 4:12, :] = own_ref[...]
    ext[8:12, 4:12, :] = choose(odd, outery_ref[...], innery_ref[...])
    odd = lax.axis_index("gx") % 2 == 1
    ext[:, 0:4, :] = choose(odd, innerx_ref[...], outerx_ref[...])
    ext[:, 12:16, :] = choose(odd, outerx_ref[...], innerx_ref[...])
    g = ext[...]
    for _ in range(GSUB):
        center = g[1:-1]
        east = jnp.stack([pltpu.roll(center[i], 15, 0) for i in range(center.shape[0])])
        west = jnp.stack([pltpu.roll(center[i], 1, 0) for i in range(center.shape[0])])
        north = g[2:]
        south = g[:-2]
        step = 0.2 * (east + west + north + south - 4.0 * center) - 0.15 * (east - west) - 0.15 * (north - south)
        g = center + 0.5 * step
    for y in range(TY):
        last = pltpu.roll(g[y], 12, 0)[:TX]
        g4_ref[y] = last
        forcing = (last - own_ref[y]) / (0.5 * GSUB)
        for x in range(TX):
            slot = assign_ref[y, x]
            rows[slot // SLOTS, pl.ds(slot & (SLOTS - 1), 1), :] = forcing[x : x + 1]
    for k, part in enumerate((f0_ref, f1_ref, f2_ref, f3_ref)):
        part[...] = rows[me ^ ORDER[k]]


def split(value):
    high = value.astype(jnp.bfloat16)
    rest = value - high.astype(jnp.float32)
    middle = rest.astype(jnp.bfloat16)
    low = (rest - middle.astype(jnp.float32)).astype(jnp.bfloat16)
    return high, middle, low


def advance_kernel(
    assign_ref,
    sub_ref,
    mix_ref,
    r0_ref,
    r1_ref,
    r2_ref,
    r3_ref,
    f0_ref,
    f1_ref,
    f2_ref,
    f3_ref,
    out_ref,
    tend_ref,
    counts,
    one,
    two,
    push,
    gather,
    held,
    weights,
    staged,
    sems,
):
    me = lax.axis_index("ha")
    for x in range(TX):
        for y in range(TY):
            counts[assign_ref[y, x]] = sub_ref[y, x]
    tend_ref[...] = jnp.zeros_like(tend_ref)
    gather[...] = jnp.zeros_like(gather)
    for h in range(FIELDS):
        for g in range(FIELDS):
            weights[h, g] = jnp.full((8, LANES), 0.1 * mix_ref[h, g], jnp.float32)
    lane8 = lax.broadcasted_iota(jnp.int32, (8, LANES), 1)
    half = lane8 & WIDTH
    to_right = half | ((lane8 + 1) & (WIDTH - 1))
    to_left = half | ((lane8 + WIDTH - 1) & (WIDTH - 1))
    slot_row = lax.broadcasted_iota(jnp.int32, (SLOTS, LANES), 0)
    slot_pair = lax.broadcasted_iota(jnp.int32, (SLOTS, LANES), 1) // WIDTH
    arrived = (r0_ref, r1_ref, r2_ref, r3_ref)
    forcings = (f0_ref, f1_ref, f2_ref, f3_ref)

    def ends(ref):
        for f in range(FIELDS):
            ref[f, BASE - 1 : BASE, :] = ref[f, BASE : BASE + 1, :]
            ref[f, BASE + LEVELS : BASE + LEVELS + 1, :] = ref[f, BASE + LEVELS - 1 : BASE + LEVELS, :]

    def send(pair, buffer):
        return pltpu.make_async_copy(
            staged.at[buffer], out_ref.at[:, pl.ds(pl.multiple_of(pair * LANES, LANES), LANES)], sems.at[buffer]
        )

    def one_pair(pair, buffer):
        first = me * SLOTS + 2 * pair
        n0 = counts[first]
        n1 = counts[first + 1]
        limit = jnp.where(lane8 < WIDTH, n0, n1)
        steps = jnp.maximum(n0, n1)
        chosen = slot_row == 2 * pair + slot_pair
        spread = jnp.where(chosen, 1.0, 0.0).astype(jnp.bfloat16)
        averaging = jnp.where(chosen, 1.0 / WIDTH, 0.0).astype(jnp.bfloat16)

        for k in range(HELP):
            terms = split(0.1 * forcings[k][...])
            total = None
            for term in terms:
                part = lax.dot_general(term, spread, (((0,), (0,)), ((), ())), preferred_element_type=jnp.float32)
                total = part if total is None else total + part
            held[k] = total
            start = (me ^ ORDER[k]) * PART
            for f in range(FIELDS):
                for i in PIECES:
                    push[f, pl.ds(start + i, 8), :] = held[k, f * PITCH + i : f * PITCH + i + 8, :]
            for f in range(FIELDS):
                for i in PIECES:
                    one[f, pl.ds(BASE + start + i, 8), :] = arrived[k][pl.ds(pair * ROWS + f * PART + i, 8), :]
        ends(one)

        def substep(source, target, index):
            active = index < limit
            for b in range(BLOCKS):
                row = BASE + 8 * b
                here = [source[f, row : row + 8, :] for f in range(FIELDS)]
                warm = [jnp.tanh(s) for s in here]
                for h in range(FIELDS):
                    s = here[h]
                    right = jnp.take_along_axis(s, to_right, axis=1)
                    left = jnp.take_along_axis(s, to_left, axis=1)
                    upper = source[h, row - 1 : row + 7, :]
                    lower = source[h, row + 1 : row + 9, :]
                    mixed = weights[h, 0] * warm[0]
                    for g in range(1, FIELDS):
                        mixed = mixed + weights[h, g] * warm[g]
                    total = 0.7 * s + push[h, 8 * b : 8 * b + 8, :]
                    total = total + 0.1 * (right + left) + 0.05 * (upper + lower)
                    target[h, row : row + 8, :] = jnp.where(active, total + mixed, s)
            ends(target)

        def twice(index, _):
            substep(one, two, 2 * index)
            substep(two, one, 2 * index + 1)
            return 0

        lax.fori_loop(0, steps // 2, twice, 0)

        @pl.when(steps % 2 == 1)
        def _():
            substep(one, two, steps - 1)
            for f in range(FIELDS):
                one[f, BASE : BASE + 64, :] = two[f, BASE : BASE + 64, :]

        for f in range(FIELDS):
            for b in range(BLOCKS):
                n = min(8, LEVELS - 8 * b)
                staged[buffer, pl.ds(8 * b * FIELDS + f, n, stride=FIELDS), :] = one[f, BASE + 8 * b : BASE + 8 * b + n, :]
        send(pair, buffer).start()
        for k in range(HELP):
            owner = me ^ ORDER[k]
            for f in range(FIELDS):
                for i in PIECES:
                    gather[f * PITCH + i : f * PITCH + i + 8, :] = (
                        one[f, pl.ds(BASE + owner * PART + i, 8), :] - arrived[k][pl.ds(pair * ROWS + f * PART + i, 8), :]
                    )
            total = None
            for term in split(gather[...]):
                part = lax.dot_general(averaging, term, (((1,), (1,)), ((), ())), preferred_element_type=jnp.float32)
                total = part if total is None else total + part
            tend_ref[owner] += total

    def each(pair, _):
        one_pair(pair, pair)
        return 0

    lax.fori_loop(0, PAIRS, each, 0)
    for pair in range(PAIRS):
        send(pair, pair).wait()


def placing_kernel(assign_ref, g4_ref, tend_ref, out_ref, rows, turned):
    for x in range(TX):
        for y in range(TY):
            rows[x * TY + y : x * TY + y + 1, :] = g4_ref[y, x : x + 1, :] + tend_ref[pl.ds(assign_ref[y, x], 1), :]
    for f in range(FIELDS):
        turned[f] = pltpu.roll(rows[...], (LANES - f * PITCH) % LANES, 1)
        for x in range(TX):
            out_ref[f, x] = turned[f, x * TY : (x + 1) * TY, :PART]


def swaps(count, first):
    pairs = [(i, (i + 1) % count) for i in range(first, count, 2)]
    return pairs + [(b, a) for a, b in pairs]


def partners(k):
    return [(i, i ^ k) for i in range(HELP)]


def on_device(global_state, crm_state, mixing, substeps, assignment):
    f32 = jnp.float32
    assignment = assignment.T
    substeps = substeps.T
    own = jnp.pad(global_state, ((0, 0), (0, PITCH - PART), (0, 0), (0, 0)))
    own = own.transpose(3, 2, 0, 1).reshape(TY, TX, LANES)
    ny = lax.axis_size("gy")
    nx = lax.axis_size("gx")
    outer = lax.ppermute(own, "gy", swaps(ny, 1))
    inner = lax.ppermute(own, "gy", swaps(ny, 0))

    slotted = pl.pallas_call(
        slotting_kernel,
        out_shape=[jax.ShapeDtypeStruct((PAIRS * ROWS, LANES), f32)] * HELP,
        in_specs=[smem(), pl.BlockSpec(memory_space=pltpu.HBM)],
        out_specs=[vmem()] * HELP,
        scratch_shapes=[
            pltpu.SMEM((COLS,), jnp.int32),
            pltpu.VMEM((TY // 2, ROWS * TX, LANES), f32),
            pltpu.SemaphoreType.DMA((TY // 2,)),
        ],
        compiler_params=pltpu.CompilerParams(vmem_limit_bytes=60 * 1024 * 1024),
    )(assignment, crm_state.reshape(ROWS * TX, TY * WIDTH))
    *slotted, outer, inner = lax.optimization_barrier((*slotted, outer, inner))
    arrived = [slotted[0]] + [lax.ppermute(slotted[k], "ha", partners(ORDER[k])) for k in range(1, HELP)]

    edge = jax.ShapeDtypeStruct((3 * TY, 4, LANES), f32)
    to_outer, to_inner = pl.pallas_call(
        border_kernel,
        out_shape=[edge, edge],
        in_specs=[vmem()] * 3,
        out_specs=[vmem()] * 2,
        scratch_shapes=[pltpu.VMEM((3 * TY, TX, LANES), f32)],
        cost_estimate=pl.CostEstimate(flops=1000, bytes_accessed=300_000, transcendentals=0),
        compiler_params=VM,
    )(own, outer, inner)
    outerx = lax.ppermute(to_outer, "gx", swaps(nx, 1))
    innerx = lax.ppermute(to_inner, "gx", swaps(nx, 0))
    rowshape = jax.ShapeDtypeStruct((SLOTS, LANES), f32)
    g4, *pushes = pl.pallas_call(
        forcing_kernel,
        out_shape=[jax.ShapeDtypeStruct((TY, TX, LANES), f32)] + [rowshape] * HELP,
        in_specs=[smem()] + [vmem()] * 5,
        out_specs=[vmem()] * 5,
        scratch_shapes=[pltpu.VMEM((12, 16, LANES), f32), pltpu.VMEM((HELP, SLOTS, LANES), f32)],
        compiler_params=VM,
    )(assignment, own, outer, inner, outerx, innerx)
    for k in range(1, HELP):
        pushes[k] = lax.ppermute(pushes[k], "ha", partners(ORDER[k]))

    final, tendency = pl.pallas_call(
        advance_kernel,
        out_shape=[
            jax.ShapeDtypeStruct((LEVELS * FIELDS, SLOTS * WIDTH), f32),
            jax.ShapeDtypeStruct((HELP, SLOTS, LANES), f32),
        ],
        in_specs=[smem(), smem(), smem()] + [vmem()] * (2 * HELP),
        out_specs=[pl.BlockSpec(memory_space=pltpu.HBM), vmem()],
        scratch_shapes=[
            pltpu.SMEM((COLS,), jnp.int32),
            pltpu.VMEM((FIELDS, SROWS, LANES), f32),
            pltpu.VMEM((FIELDS, SROWS, LANES), f32),
            pltpu.VMEM((FIELDS, 64, LANES), f32),
            pltpu.VMEM((FIELDS * PITCH, LANES), f32),
            pltpu.VMEM((HELP, FIELDS * PITCH, LANES), f32),
            pltpu.VMEM((FIELDS, FIELDS, 8, LANES), f32),
            pltpu.VMEM((PAIRS, LEVELS * FIELDS, LANES), f32),
            pltpu.SemaphoreType.DMA((PAIRS,)),
        ],
        compiler_params=VM,
    )(assignment, substeps, mixing, *arrived, *pushes)
    returned = lax.all_to_all(tendency, "ha", split_axis=0, concat_axis=0, tiled=True)
    placed = pl.pallas_call(
        placing_kernel,
        out_shape=jax.ShapeDtypeStruct((FIELDS, TX, TY, PART), f32),
        in_specs=[smem(), vmem(), vmem()],
        out_specs=vmem(),
        scratch_shapes=[pltpu.VMEM((COLS, LANES), f32), pltpu.VMEM((FIELDS, COLS, LANES), f32)],
        compiler_params=VM,
    )(assignment, g4, returned.reshape(COLS, LANES))
    new_global = placed.transpose(0, 3, 1, 2)
    new_crm = final.reshape(LEVELS, FIELDS, SLOTS * WIDTH).transpose(1, 0, 2)
    return new_global, new_crm


def solution(mesh):
    in_specs = (
        P(None, "ha", "gx", "gy"),
        P(None, "ha", "gx", "gy"),
        P(),
        P("gx", "gy"),
        P("gx", "gy"),
    )
    out_specs = (P(None, "ha", "gx", "gy"), P(None, None, ("gx", "gy", "ha")))
    return jax.shard_map(
        on_device, mesh=mesh, in_specs=in_specs, out_specs=out_specs, check_vma=False
    )
```

```python
import jax
import jax.numpy as jnp
from jax import lax
from jax.experimental import pallas as pl
from jax.experimental.pallas import tpu as pltpu
from jax.sharding import PartitionSpec as P

MAXSUB = 8
GSUB = 4
FIELDS = 8
PART = 15
ROWS = FIELDS * PART
PITCH = 16
LANES = 128
WIDTH = 64
TX = 8
TY = 4
COLS = TX * TY
HELP = 4
ORDER = (0, 1, 3, 2)
SLOTS = 8
PAIRS = SLOTS // 2
LEVELS = PART * HELP
BASE = 8
SROWS = 80
BLOCKS = 8
PIECES = (0, PART - 8)

VM = pltpu.CompilerParams(vmem_limit_bytes=32 * 1024 * 1024)


def smem():
    return pl.BlockSpec(memory_space=pltpu.SMEM)


def vmem():
    return pl.BlockSpec(memory_space=pltpu.VMEM)


def slotting_kernel(assign_ref, crm_ref, s0_ref, s1_ref, s2_ref, s3_ref, inverse, held, sems):
    me = lax.axis_index("ha")
    loads = [
        pltpu.make_async_copy(crm_ref.at[:, i * LANES : (i + 1) * LANES], held.at[i], sems.at[i]) for i in range(TY // 2)
    ]
    for load in loads:
        load.start()
    for x in range(TX):
        for y in range(TY):
            inverse[assign_ref[y, x]] = x * TY + y
    lane = lax.broadcasted_iota(jnp.int32, (ROWS, LANES), 1)

    def column(slot, half):
        place = inverse[slot]
        x = place // TY
        y = place % TY
        rows = held[y // 2, pl.ds(x, ROWS, stride=TX), :]
        return pltpu.roll(rows, ((y % 2) ^ half) * WIDTH, 1)

    for load in loads:
        load.wait()
    for k, part in enumerate((s0_ref, s1_ref, s2_ref, s3_ref)):
        for pair in range(PAIRS):
            slot = (me ^ ORDER[k]) * SLOTS + 2 * pair
            part[pair * ROWS : (pair + 1) * ROWS, :] = jnp.where(lane < WIDTH, column(slot, 0), column(slot + 1, 1))


def choose(odd, first, second):
    return jnp.where(odd, first, second)


def border_kernel(own_ref, outer_ref, inner_ref, to_outer_ref, to_inner_ref, tall):
    odd = lax.axis_index("gy") % 2 == 1
    tall[0:4] = choose(odd, inner_ref[...], outer_ref[...])
    tall[4:8] = own_ref[...]
    tall[8:12] = choose(odd, outer_ref[...], inner_ref[...])
    odd = lax.axis_index("gx") % 2 == 1
    low, high = tall[:, 0:4, :], tall[:, TX - 4 : TX, :]
    to_outer_ref[...] = choose(odd, high, low)
    to_inner_ref[...] = choose(odd, low, high)


def forcing_kernel(assign_ref, own_ref, outery_ref, innery_ref, outerx_ref, innerx_ref, g4_ref, rows_ref, ext):
    odd = lax.axis_index("gy") % 2 == 1
    ext[0:4, 4:12, :] = choose(odd, innery_ref[...], outery_ref[...])
    ext[4:8, 4:12, :] = own_ref[...]
    ext[8:12, 4:12, :] = choose(odd, outery_ref[...], innery_ref[...])
    odd = lax.axis_index("gx") % 2 == 1
    ext[:, 0:4, :] = choose(odd, innerx_ref[...], outerx_ref[...])
    ext[:, 12:16, :] = choose(odd, outerx_ref[...], innerx_ref[...])
    g = ext[...]
    for _ in range(GSUB):
        center = g[1:-1]
        east = jnp.stack([pltpu.roll(center[i], 15, 0) for i in range(center.shape[0])])
        west = jnp.stack([pltpu.roll(center[i], 1, 0) for i in range(center.shape[0])])
        north = g[2:]
        south = g[:-2]
        step = 0.2 * (east + west + north + south - 4.0 * center) - 0.15 * (east - west) - 0.15 * (north - south)
        g = center + 0.5 * step
    for y in range(TY):
        last = pltpu.roll(g[y], 12, 0)[:TX]
        g4_ref[y] = last
        forcing = (last - own_ref[y]) / (0.5 * GSUB)
        for x in range(TX):
            slot = assign_ref[y, x]
            rows_ref[slot // SLOTS, pl.ds(slot & (SLOTS - 1), 1), :] = forcing[x : x + 1]


def split(value):
    high = value.astype(jnp.bfloat16)
    rest = value - high.astype(jnp.float32)
    middle = rest.astype(jnp.bfloat16)
    low = (rest - middle.astype(jnp.float32)).astype(jnp.bfloat16)
    return high, middle, low


def advance_kernel(
    assign_ref,
    sub_ref,
    mix_ref,
    r0_ref,
    r1_ref,
    r2_ref,
    r3_ref,
    push_ref,
    out_ref,
    tend_ref,
    counts,
    one,
    two,
    push,
    gather,
    held,
    weights,
    staged,
    mine,
    sems,
):
    load = pltpu.make_async_copy(r0_ref, mine, sems.at[PAIRS])
    load.start()
    me = lax.axis_index("ha")
    for x in range(TX):
        for y in range(TY):
            counts[assign_ref[y, x]] = sub_ref[y, x]
    tend_ref[...] = jnp.zeros_like(tend_ref)
    gather[...] = jnp.zeros_like(gather)
    for h in range(FIELDS):
        for g in range(FIELDS):
            weights[h, g] = jnp.full((8, LANES), 0.1 * mix_ref[h, g], jnp.float32)
    lane8 = lax.broadcasted_iota(jnp.int32, (8, LANES), 1)
    half = lane8 & WIDTH
    to_right = half | ((lane8 + 1) & (WIDTH - 1))
    to_left = half | ((lane8 + WIDTH - 1) & (WIDTH - 1))
    slot_row = lax.broadcasted_iota(jnp.int32, (SLOTS, LANES), 0)
    slot_pair = lax.broadcasted_iota(jnp.int32, (SLOTS, LANES), 1) // WIDTH
    arrived = (mine, r1_ref, r2_ref, r3_ref)

    def ends(ref):
        for f in range(FIELDS):
            ref[f, BASE - 1 : BASE, :] = ref[f, BASE : BASE + 1, :]
            ref[f, BASE + LEVELS : BASE + LEVELS + 1, :] = ref[f, BASE + LEVELS - 1 : BASE + LEVELS, :]

    def send(pair, buffer):
        return pltpu.make_async_copy(
            staged.at[buffer], out_ref.at[:, pl.ds(pl.multiple_of(pair * LANES, LANES), LANES)], sems.at[buffer]
        )

    def one_pair(pair, buffer):
        first = me * SLOTS + 2 * pair
        n0 = counts[first]
        n1 = counts[first + 1]
        limit = jnp.where(lane8 < WIDTH, n0, n1)
        steps = jnp.maximum(n0, n1)
        chosen = slot_row == 2 * pair + slot_pair
        spread = jnp.where(chosen, 1.0, 0.0).astype(jnp.bfloat16)
        averaging = jnp.where(chosen, 1.0 / WIDTH, 0.0).astype(jnp.bfloat16)

        for k in range(HELP):
            terms = split(0.1 * push_ref[k])
            total = None
            for term in terms:
                part = lax.dot_general(term, spread, (((0,), (0,)), ((), ())), preferred_element_type=jnp.float32)
                total = part if total is None else total + part
            held[k] = total
            start = (me ^ ORDER[k]) * PART
            for f in range(FIELDS):
                for i in PIECES:
                    push[f, k * PART + i : k * PART + i + 8, :] = held[k, f * PITCH + i : f * PITCH + i + 8, :]
            for f in range(FIELDS):
                for i in PIECES:
                    one[f, pl.ds(BASE + start + i, 8), :] = arrived[k][pl.ds(pair * ROWS + f * PART + i, 8), :]
        ends(one)

        def substep(source, target, index):
            active = index < limit
            for b in range(BLOCKS):
                row = BASE + 8 * b
                here = [source[f, row : row + 8, :] for f in range(FIELDS)]
                warm = [jnp.tanh(s) for s in here]
                for h in range(FIELDS):
                    s = here[h]
                    right = jnp.take_along_axis(s, to_right, axis=1)
                    left = jnp.take_along_axis(s, to_left, axis=1)
                    upper = source[h, row - 1 : row + 7, :]
                    lower = source[h, row + 1 : row + 9, :]
                    mixed = weights[h, 0] * warm[0]
                    for g in range(1, FIELDS):
                        mixed = mixed + weights[h, g] * warm[g]
                    total = 0.7 * s + push[h, 8 * b : 8 * b + 8, :]
                    total = total + 0.1 * (right + left) + 0.05 * (upper + lower)
                    target[h, row : row + 8, :] = jnp.where(active, total + mixed, s)
            ends(target)

        def twice(index, _):
            substep(one, two, 2 * index)
            substep(two, one, 2 * index + 1)
            return 0

        lax.fori_loop(0, steps // 2, twice, 0)

        @pl.when(steps % 2 == 1)
        def _():
            substep(one, two, steps - 1)
            for f in range(FIELDS):
                one[f, BASE : BASE + 64, :] = two[f, BASE : BASE + 64, :]

        for f in range(FIELDS):
            for b in range(BLOCKS):
                n = min(8, LEVELS - 8 * b)
                staged[buffer, pl.ds(8 * b * FIELDS + f, n, stride=FIELDS), :] = one[f, BASE + 8 * b : BASE + 8 * b + n, :]
        send(pair, buffer).start()
        for k in range(HELP):
            owner = me ^ ORDER[k]
            for f in range(FIELDS):
                for i in PIECES:
                    gather[f * PITCH + i : f * PITCH + i + 8, :] = (
                        one[f, pl.ds(BASE + owner * PART + i, 8), :] - arrived[k][pl.ds(pair * ROWS + f * PART + i, 8), :]
                    )
            total = None
            for term in split(gather[...]):
                part = lax.dot_general(averaging, term, (((1,), (1,)), ((), ())), preferred_element_type=jnp.float32)
                total = part if total is None else total + part
            tend_ref[owner] += total

    def each(pair, _):
        one_pair(pair, pair)
        return 0

    load.wait()
    lax.fori_loop(0, PAIRS, each, 0)
    for pair in range(PAIRS):
        send(pair, pair).wait()


def placing_kernel(assign_ref, g4_ref, tend_ref, out_ref, rows, turned):
    for x in range(TX):
        for y in range(TY):
            rows[x * TY + y : x * TY + y + 1, :] = g4_ref[y, x : x + 1, :] + tend_ref[pl.ds(assign_ref[y, x], 1), :]
    for f in range(FIELDS):
        turned[f] = pltpu.roll(rows[...], (LANES - f * PITCH) % LANES, 1)
        for x in range(TX):
            out_ref[f, x] = turned[f, x * TY : (x + 1) * TY, :PART]


def swaps(count, first):
    pairs = [(i, (i + 1) % count) for i in range(first, count, 2)]
    return pairs + [(b, a) for a, b in pairs]


def partners(k):
    return [(i, i ^ k) for i in range(HELP)]


def on_device(global_state, crm_state, mixing, substeps, assignment):
    f32 = jnp.float32
    assignment = assignment.T
    substeps = substeps.T
    own = jnp.pad(global_state, ((0, 0), (0, PITCH - PART), (0, 0), (0, 0)))
    own = own.transpose(3, 2, 0, 1).reshape(TY, TX, LANES)
    ny = lax.axis_size("gy")
    nx = lax.axis_size("gx")
    outer = lax.ppermute(own, "gy", swaps(ny, 1))
    inner = lax.ppermute(own, "gy", swaps(ny, 0))

    slotted = pl.pallas_call(
        slotting_kernel,
        out_shape=[jax.ShapeDtypeStruct((PAIRS * ROWS, LANES), f32)] * HELP,
        in_specs=[smem(), pl.BlockSpec(memory_space=pltpu.HBM)],
        out_specs=[vmem()] * HELP,
        scratch_shapes=[
            pltpu.SMEM((COLS,), jnp.int32),
            pltpu.VMEM((TY // 2, ROWS * TX, LANES), f32),
            pltpu.SemaphoreType.DMA((TY // 2,)),
        ],
        compiler_params=pltpu.CompilerParams(vmem_limit_bytes=60 * 1024 * 1024),
    )(assignment, crm_state.reshape(ROWS * TX, TY * WIDTH))
    *slotted, outer = lax.optimization_barrier((*slotted, outer))
    arrived = [slotted[0]] + [lax.ppermute(slotted[k], "ha", partners(ORDER[k])) for k in range(1, HELP)]

    edge = jax.ShapeDtypeStruct((3 * TY, 4, LANES), f32)
    to_outer, to_inner = pl.pallas_call(
        border_kernel,
        out_shape=[edge, edge],
        in_specs=[vmem()] * 3,
        out_specs=[vmem()] * 2,
        scratch_shapes=[pltpu.VMEM((3 * TY, TX, LANES), f32)],
        cost_estimate=pl.CostEstimate(flops=1000, bytes_accessed=300_000, transcendentals=0),
        compiler_params=VM,
    )(own, outer, inner)
    outerx = lax.ppermute(to_outer, "gx", swaps(nx, 1))
    innerx = lax.ppermute(to_inner, "gx", swaps(nx, 0))
    g4, pushes = pl.pallas_call(
        forcing_kernel,
        out_shape=[
            jax.ShapeDtypeStruct((TY, TX, LANES), f32),
            jax.ShapeDtypeStruct((HELP, SLOTS, LANES), f32),
        ],
        in_specs=[smem()] + [vmem()] * 5,
        out_specs=[vmem()] * 2,
        scratch_shapes=[pltpu.VMEM((12, 16, LANES), f32)],
        compiler_params=VM,
    )(assignment, own, outer, inner, outerx, innerx)
    pushes = lax.all_to_all(pushes, "ha", split_axis=0, concat_axis=0, tiled=True)

    final, tendency = pl.pallas_call(
        advance_kernel,
        out_shape=[
            jax.ShapeDtypeStruct((LEVELS * FIELDS, SLOTS * WIDTH), f32),
            jax.ShapeDtypeStruct((HELP, SLOTS, LANES), f32),
        ],
        in_specs=[smem(), smem(), smem()] + [pl.BlockSpec(memory_space=pltpu.HBM)] + [vmem()] * HELP,
        out_specs=[pl.BlockSpec(memory_space=pltpu.HBM), vmem()],
        scratch_shapes=[
            pltpu.SMEM((COLS,), jnp.int32),
            pltpu.VMEM((FIELDS, SROWS, LANES), f32),
            pltpu.VMEM((FIELDS, SROWS, LANES), f32),
            pltpu.VMEM((FIELDS, 64, LANES), f32),
            pltpu.VMEM((FIELDS * PITCH, LANES), f32),
            pltpu.VMEM((HELP, FIELDS * PITCH, LANES), f32),
            pltpu.VMEM((FIELDS, FIELDS, 8, LANES), f32),
            pltpu.VMEM((PAIRS, LEVELS * FIELDS, LANES), f32),
            pltpu.VMEM((PAIRS * ROWS, LANES), f32),
            pltpu.SemaphoreType.DMA((PAIRS + 1,)),
        ],
        compiler_params=VM,
    )(assignment, substeps, mixing, *arrived, pushes)
    returned = lax.all_to_all(tendency, "ha", split_axis=0, concat_axis=0, tiled=True)
    placed = pl.pallas_call(
        placing_kernel,
        out_shape=jax.ShapeDtypeStruct((FIELDS, TX, TY, PART), f32),
        in_specs=[smem(), vmem(), vmem()],
        out_specs=vmem(),
        scratch_shapes=[pltpu.VMEM((COLS, LANES), f32), pltpu.VMEM((FIELDS, COLS, LANES), f32)],
        compiler_params=VM,
    )(assignment, g4, returned.reshape(COLS, LANES))
    new_global = placed.transpose(0, 3, 1, 2)
    new_crm = final.reshape(LEVELS, FIELDS, SLOTS * WIDTH).transpose(1, 0, 2)
    return new_global, new_crm


def solution(mesh):
    in_specs = (
        P(None, "ha", "gx", "gy"),
        P(None, "ha", "gx", "gy"),
        P(),
        P("gx", "gy"),
        P("gx", "gy"),
    )
    out_specs = (P(None, "ha", "gx", "gy"), P(None, None, ("gx", "gy", "ha")))
    return jax.shard_map(
        on_device, mesh=mesh, in_specs=in_specs, out_specs=out_specs, check_vma=False
    )
```

```python
import jax
import jax.numpy as jnp
from jax import lax
from jax.experimental import pallas as pl
from jax.experimental.pallas import tpu as pltpu
from jax.sharding import PartitionSpec as P

MAXSUB = 8
GSUB = 4
FIELDS = 8
PART = 15
ROWS = FIELDS * PART
PITCH = 16
LANES = 128
WIDTH = 64
TX = 8
TY = 4
COLS = TX * TY
HELP = 4
ORDER = (0, 2, 1, 3)
SLOTS = 8
PAIRS = SLOTS // 2
LEVELS = PART * HELP
BASE = 8
SROWS = 80
BLOCKS = 8
PIECES = (0, PART - 8)

VM = pltpu.CompilerParams(vmem_limit_bytes=32 * 1024 * 1024)


def smem():
    return pl.BlockSpec(memory_space=pltpu.SMEM)


def vmem():
    return pl.BlockSpec(memory_space=pltpu.VMEM)


def slotting_kernel(assign_ref, crm_ref, s0_ref, s1_ref, s2_ref, s3_ref, inverse, held, sems):
    me = lax.axis_index("ha")
    loads = [
        pltpu.make_async_copy(crm_ref.at[:, i * LANES : (i + 1) * LANES], held.at[i], sems.at[i]) for i in range(TY // 2)
    ]
    for load in loads:
        load.start()
    for x in range(TX):
        for y in range(TY):
            inverse[assign_ref[y, x]] = x * TY + y
    lane = lax.broadcasted_iota(jnp.int32, (ROWS, LANES), 1)

    def column(slot, half):
        place = inverse[slot]
        x = place // TY
        y = place % TY
        rows = held[y // 2, pl.ds(x, ROWS, stride=TX), :]
        return pltpu.roll(rows, ((y % 2) ^ half) * WIDTH, 1)

    for load in loads:
        load.wait()
    for k, part in enumerate((s0_ref, s1_ref, s2_ref, s3_ref)):
        for pair in range(PAIRS):
            slot = (me ^ ORDER[k]) * SLOTS + 2 * pair
            part[pair * ROWS : (pair + 1) * ROWS, :] = jnp.where(lane < WIDTH, column(slot, 0), column(slot + 1, 1))


def choose(odd, first, second):
    return jnp.where(odd, first, second)


def border_kernel(own_ref, outer_ref, inner_ref, to_outer_ref, to_inner_ref, tall):
    odd = lax.axis_index("gy") % 2 == 1
    tall[0:4] = choose(odd, inner_ref[...], outer_ref[...])
    tall[4:8] = own_ref[...]
    tall[8:12] = choose(odd, outer_ref[...], inner_ref[...])
    odd = lax.axis_index("gx") % 2 == 1
    low, high = tall[:, 0:4, :], tall[:, TX - 4 : TX, :]
    to_outer_ref[...] = choose(odd, high, low)
    to_inner_ref[...] = choose(odd, low, high)


def forcing_kernel(assign_ref, own_ref, outery_ref, innery_ref, outerx_ref, innerx_ref, s0_ref, g4_ref, rows_ref, mine_ref, ext, sem):
    load = pltpu.make_async_copy(s0_ref, mine_ref, sem)
    load.start()
    odd = lax.axis_index("gy") % 2 == 1
    ext[0:4, 4:12, :] = choose(odd, innery_ref[...], outery_ref[...])
    ext[4:8, 4:12, :] = own_ref[...]
    ext[8:12, 4:12, :] = choose(odd, outery_ref[...], innery_ref[...])
    odd = lax.axis_index("gx") % 2 == 1
    ext[:, 0:4, :] = choose(odd, innerx_ref[...], outerx_ref[...])
    ext[:, 12:16, :] = choose(odd, outerx_ref[...], innerx_ref[...])
    g = ext[...]
    for _ in range(GSUB):
        center = g[1:-1]
        east = jnp.stack([pltpu.roll(center[i], 15, 0) for i in range(center.shape[0])])
        west = jnp.stack([pltpu.roll(center[i], 1, 0) for i in range(center.shape[0])])
        north = g[2:]
        south = g[:-2]
        step = 0.2 * (east + west + north + south - 4.0 * center) - 0.15 * (east - west) - 0.15 * (north - south)
        g = center + 0.5 * step
    for y in range(TY):
        last = pltpu.roll(g[y], 12, 0)[:TX]
        g4_ref[y] = last
        forcing = (last - own_ref[y]) / (0.5 * GSUB)
        for x in range(TX):
            slot = assign_ref[y, x]
            rows_ref[slot // SLOTS, pl.ds(slot & (SLOTS - 1), 1), :] = forcing[x : x + 1]
    load.wait()


def split(value):
    high = value.astype(jnp.bfloat16)
    rest = value - high.astype(jnp.float32)
    middle = rest.astype(jnp.bfloat16)
    low = (rest - middle.astype(jnp.float32)).astype(jnp.bfloat16)
    return high, middle, low


def advance_kernel(
    assign_ref,
    sub_ref,
    mix_ref,
    r0_ref,
    r1_ref,
    r2_ref,
    r3_ref,
    push_ref,
    out_ref,
    tend_ref,
    counts,
    one,
    two,
    push,
    gather,
    held,
    weights,
    staged,
    sems,
):
    me = lax.axis_index("ha")
    for x in range(TX):
        for y in range(TY):
            counts[assign_ref[y, x]] = sub_ref[y, x]
    tend_ref[...] = jnp.zeros_like(tend_ref)
    gather[...] = jnp.zeros_like(gather)
    for h in range(FIELDS):
        for g in range(FIELDS):
            weights[h, g] = jnp.full((8, LANES), 0.1 * mix_ref[h, g], jnp.float32)
    lane8 = lax.broadcasted_iota(jnp.int32, (8, LANES), 1)
    half = lane8 & WIDTH
    to_right = half | ((lane8 + 1) & (WIDTH - 1))
    to_left = half | ((lane8 + WIDTH - 1) & (WIDTH - 1))
    slot_row = lax.broadcasted_iota(jnp.int32, (SLOTS, LANES), 0)
    slot_pair = lax.broadcasted_iota(jnp.int32, (SLOTS, LANES), 1) // WIDTH
    arrived = (r0_ref, r1_ref, r2_ref, r3_ref)

    def ends(ref):
        for f in range(FIELDS):
            ref[f, BASE - 1 : BASE, :] = ref[f, BASE : BASE + 1, :]
            ref[f, BASE + LEVELS : BASE + LEVELS + 1, :] = ref[f, BASE + LEVELS - 1 : BASE + LEVELS, :]

    def send(pair, buffer):
        return pltpu.make_async_copy(
            staged.at[buffer], out_ref.at[:, pl.ds(pl.multiple_of(pair * LANES, LANES), LANES)], sems.at[buffer]
        )

    def one_pair(pair, buffer):
        first = me * SLOTS + 2 * pair
        n0 = counts[first]
        n1 = counts[first + 1]
        limit = jnp.where(lane8 < WIDTH, n0, n1)
        steps = jnp.maximum(n0, n1)
        chosen = slot_row == 2 * pair + slot_pair
        spread = jnp.where(chosen, 1.0, 0.0).astype(jnp.bfloat16)
        averaging = jnp.where(chosen, 1.0 / WIDTH, 0.0).astype(jnp.bfloat16)

        for k in range(HELP):
            terms = split(0.1 * push_ref[k])
            total = None
            for term in terms:
                part = lax.dot_general(term, spread, (((0,), (0,)), ((), ())), preferred_element_type=jnp.float32)
                total = part if total is None else total + part
            held[k] = total
            start = (me ^ ORDER[k]) * PART
            for f in range(FIELDS):
                for i in PIECES:
                    push[f, k * PART + i : k * PART + i + 8, :] = held[k, f * PITCH + i : f * PITCH + i + 8, :]
            for f in range(FIELDS):
                for i in PIECES:
                    one[f, pl.ds(BASE + start + i, 8), :] = arrived[k][pl.ds(pair * ROWS + f * PART + i, 8), :]
        ends(one)

        def substep(source, target, index):
            active = index < limit
            for b in range(BLOCKS):
                row = BASE + 8 * b
                here = [source[f, row : row + 8, :] for f in range(FIELDS)]
                warm = [jnp.tanh(s) for s in here]
                for h in range(FIELDS):
                    s = here[h]
                    right = jnp.take_along_axis(s, to_right, axis=1)
                    left = jnp.take_along_axis(s, to_left, axis=1)
                    upper = source[h, row - 1 : row + 7, :]
                    lower = source[h, row + 1 : row + 9, :]
                    mixed = weights[h, 0] * warm[0]
                    for g in range(1, FIELDS):
                        mixed = mixed + weights[h, g] * warm[g]
                    total = 0.7 * s + push[h, 8 * b : 8 * b + 8, :]
                    total = total + 0.1 * (right + left) + 0.05 * (upper + lower)
                    target[h, row : row + 8, :] = jnp.where(active, total + mixed, s)
            ends(target)

        def twice(index, _):
            substep(one, two, 2 * index)
            substep(two, one, 2 * index + 1)
            return 0

        lax.fori_loop(0, steps // 2, twice, 0)

        @pl.when(steps % 2 == 1)
        def _():
            substep(one, two, steps - 1)
            for f in range(FIELDS):
                one[f, BASE : BASE + 64, :] = two[f, BASE : BASE + 64, :]

        for f in range(FIELDS):
            for b in range(BLOCKS):
                n = min(8, LEVELS - 8 * b)
                staged[buffer, pl.ds(8 * b * FIELDS + f, n, stride=FIELDS), :] = one[f, BASE + 8 * b : BASE + 8 * b + n, :]
        send(pair, buffer).start()
        for k in range(HELP):
            owner = me ^ ORDER[k]
            for f in range(FIELDS):
                for i in PIECES:
                    gather[f * PITCH + i : f * PITCH + i + 8, :] = (
                        one[f, pl.ds(BASE + owner * PART + i, 8), :] - arrived[k][pl.ds(pair * ROWS + f * PART + i, 8), :]
                    )
            total = None
            for term in split(gather[...]):
                part = lax.dot_general(averaging, term, (((1,), (1,)), ((), ())), preferred_element_type=jnp.float32)
                total = part if total is None else total + part
            tend_ref[owner] += total

    def each(pair, _):
        one_pair(pair, pair)
        return 0

    lax.fori_loop(0, PAIRS, each, 0)
    for pair in range(PAIRS):
        send(pair, pair).wait()


def placing_kernel(assign_ref, g4_ref, tend_ref, out_ref, rows, turned):
    for x in range(TX):
        for y in range(TY):
            rows[x * TY + y : x * TY + y + 1, :] = g4_ref[y, x : x + 1, :] + tend_ref[pl.ds(assign_ref[y, x], 1), :]
    for f in range(FIELDS):
        turned[f] = pltpu.roll(rows[...], (LANES - f * PITCH) % LANES, 1)
        for x in range(TX):
            out_ref[f, x] = turned[f, x * TY : (x + 1) * TY, :PART]


def swaps(count, first):
    pairs = [(i, (i + 1) % count) for i in range(first, count, 2)]
    return pairs + [(b, a) for a, b in pairs]


def partners(k):
    return [(i, i ^ k) for i in range(HELP)]


def on_device(global_state, crm_state, mixing, substeps, assignment):
    f32 = jnp.float32
    assignment = assignment.T
    substeps = substeps.T
    own = jnp.pad(global_state, ((0, 0), (0, PITCH - PART), (0, 0), (0, 0)))
    own = own.transpose(3, 2, 0, 1).reshape(TY, TX, LANES)
    ny = lax.axis_size("gy")
    nx = lax.axis_size("gx")
    outer = lax.ppermute(own, "gy", swaps(ny, 1))
    inner = lax.ppermute(own, "gy", swaps(ny, 0))

    slotted = pl.pallas_call(
        slotting_kernel,
        out_shape=[jax.ShapeDtypeStruct((PAIRS * ROWS, LANES), f32)] * HELP,
        in_specs=[smem(), pl.BlockSpec(memory_space=pltpu.HBM)],
        out_specs=[vmem()] * HELP,
        scratch_shapes=[
            pltpu.SMEM((COLS,), jnp.int32),
            pltpu.VMEM((TY // 2, ROWS * TX, LANES), f32),
            pltpu.SemaphoreType.DMA((TY // 2,)),
        ],
        compiler_params=pltpu.CompilerParams(vmem_limit_bytes=60 * 1024 * 1024),
    )(assignment, crm_state.reshape(ROWS * TX, TY * WIDTH))
    *slotted, outer, inner = lax.optimization_barrier((*slotted, outer, inner))
    arrived = [lax.ppermute(slotted[k], "ha", partners(ORDER[k])) for k in range(1, HELP)]

    edge = jax.ShapeDtypeStruct((3 * TY, 4, LANES), f32)
    to_outer, to_inner = pl.pallas_call(
        border_kernel,
        out_shape=[edge, edge],
        in_specs=[vmem()] * 3,
        out_specs=[vmem()] * 2,
        scratch_shapes=[pltpu.VMEM((3 * TY, TX, LANES), f32)],
        cost_estimate=pl.CostEstimate(flops=1000, bytes_accessed=300_000, transcendentals=0),
        compiler_params=VM,
    )(own, outer, inner)
    outerx = lax.ppermute(to_outer, "gx", swaps(nx, 1))
    innerx = lax.ppermute(to_inner, "gx", swaps(nx, 0))
    g4, pushes, mine = pl.pallas_call(
        forcing_kernel,
        out_shape=[
            jax.ShapeDtypeStruct((TY, TX, LANES), f32),
            jax.ShapeDtypeStruct((HELP, SLOTS, LANES), f32),
            jax.ShapeDtypeStruct((PAIRS * ROWS, LANES), f32),
        ],
        in_specs=[smem()] + [vmem()] * 5 + [pl.BlockSpec(memory_space=pltpu.HBM)],
        out_specs=[vmem()] * 3,
        scratch_shapes=[pltpu.VMEM((12, 16, LANES), f32), pltpu.SemaphoreType.DMA],
        compiler_params=VM,
    )(assignment, own, outer, inner, outerx, innerx, slotted[0])
    pushes = lax.all_to_all(pushes, "ha", split_axis=0, concat_axis=0, tiled=True)

    final, tendency = pl.pallas_call(
        advance_kernel,
        out_shape=[
            jax.ShapeDtypeStruct((LEVELS * FIELDS, SLOTS * WIDTH), f32),
            jax.ShapeDtypeStruct((HELP, SLOTS, LANES), f32),
        ],
        in_specs=[smem(), smem(), smem()] + [vmem()] * (HELP + 1),
        out_specs=[pl.BlockSpec(memory_space=pltpu.HBM), vmem()],
        scratch_shapes=[
            pltpu.SMEM((COLS,), jnp.int32),
            pltpu.VMEM((FIELDS, SROWS, LANES), f32),
            pltpu.VMEM((FIELDS, SROWS, LANES), f32),
            pltpu.VMEM((FIELDS, 64, LANES), f32),
            pltpu.VMEM((FIELDS * PITCH, LANES), f32),
            pltpu.VMEM((HELP, FIELDS * PITCH, LANES), f32),
            pltpu.VMEM((FIELDS, FIELDS, 8, LANES), f32),
            pltpu.VMEM((PAIRS, LEVELS * FIELDS, LANES), f32),
            pltpu.SemaphoreType.DMA((PAIRS,)),
        ],
        compiler_params=VM,
    )(assignment, substeps, mixing, mine, *arrived, pushes)
    returned = lax.all_to_all(tendency, "ha", split_axis=0, concat_axis=0, tiled=True)
    placed = pl.pallas_call(
        placing_kernel,
        out_shape=jax.ShapeDtypeStruct((FIELDS, TX, TY, PART), f32),
        in_specs=[smem(), vmem(), vmem()],
        out_specs=vmem(),
        scratch_shapes=[pltpu.VMEM((COLS, LANES), f32), pltpu.VMEM((FIELDS, COLS, LANES), f32)],
        compiler_params=VM,
    )(assignment, g4, returned.reshape(COLS, LANES))
    new_global = placed.transpose(0, 3, 1, 2)
    new_crm = final.reshape(LEVELS, FIELDS, SLOTS * WIDTH).transpose(1, 0, 2)
    return new_global, new_crm


def solution(mesh):
    in_specs = (
        P(None, "ha", "gx", "gy"),
        P(None, "ha", "gx", "gy"),
        P(),
        P("gx", "gy"),
        P("gx", "gy"),
    )
    out_specs = (P(None, "ha", "gx", "gy"), P(None, None, ("gx", "gy", "ha")))
    return jax.shard_map(
        on_device, mesh=mesh, in_specs=in_specs, out_specs=out_specs, check_vma=False
    )
```

```python
import jax
import jax.numpy as jnp
from jax import lax
from jax.experimental import pallas as pl
from jax.experimental.pallas import tpu as pltpu
from jax.sharding import PartitionSpec as P

MAXSUB = 8
GSUB = 4
FIELDS = 8
PART = 15
ROWS = FIELDS * PART
PITCH = 16
LANES = 128
WIDTH = 64
TX = 8
TY = 4
COLS = TX * TY
HELP = 4
ORDER = (0, 2, 1, 3)
SLOTS = 8
PAIRS = SLOTS // 2
LEVELS = PART * HELP
BASE = 8
SROWS = 80
BLOCKS = 8
PIECES = (0, PART - 8)

VM = pltpu.CompilerParams(vmem_limit_bytes=32 * 1024 * 1024)


def smem():
    return pl.BlockSpec(memory_space=pltpu.SMEM)


def vmem():
    return pl.BlockSpec(memory_space=pltpu.VMEM)


def slotting_kernel(assign_ref, crm_ref, s0_ref, s1_ref, s2_ref, s3_ref, inverse, held, sems):
    me = lax.axis_index("ha")
    loads = [
        pltpu.make_async_copy(crm_ref.at[:, i * LANES : (i + 1) * LANES], held.at[i], sems.at[i]) for i in range(TY // 2)
    ]
    for load in loads:
        load.start()
    for x in range(TX):
        for y in range(TY):
            inverse[assign_ref[y, x]] = x * TY + y
    lane = lax.broadcasted_iota(jnp.int32, (ROWS, LANES), 1)

    def column(slot, half):
        place = inverse[slot]
        x = place // TY
        y = place % TY
        rows = held[y // 2, pl.ds(x, ROWS, stride=TX), :]
        return pltpu.roll(rows, ((y % 2) ^ half) * WIDTH, 1)

    for load in loads:
        load.wait()
    for k, part in enumerate((s0_ref, s1_ref, s2_ref, s3_ref)):
        for pair in range(PAIRS):
            slot = (me ^ ORDER[k]) * SLOTS + 2 * pair
            part[pair * ROWS : (pair + 1) * ROWS, :] = jnp.where(lane < WIDTH, column(slot, 0), column(slot + 1, 1))


def choose(odd, first, second):
    return jnp.where(odd, first, second)


def border_kernel(own_ref, outer_ref, inner_ref, to_outer_ref, to_inner_ref, tall):
    odd = lax.axis_index("gy") % 2 == 1
    tall[0:4] = choose(odd, inner_ref[...], outer_ref[...])
    tall[4:8] = own_ref[...]
    tall[8:12] = choose(odd, outer_ref[...], inner_ref[...])
    odd = lax.axis_index("gx") % 2 == 1
    low, high = tall[:, 0:4, :], tall[:, TX - 4 : TX, :]
    to_outer_ref[...] = choose(odd, high, low)
    to_inner_ref[...] = choose(odd, low, high)


def forcing_kernel(assign_ref, sub_ref, own_ref, outery_ref, innery_ref, outerx_ref, innerx_ref, s0_ref, g4_ref, rows_ref, mine_ref, counts_ref, ext, sem):
    load = pltpu.make_async_copy(s0_ref, mine_ref, sem)
    load.start()
    odd = lax.axis_index("gy") % 2 == 1
    ext[0:4, 4:12, :] = choose(odd, innery_ref[...], outery_ref[...])
    ext[4:8, 4:12, :] = own_ref[...]
    ext[8:12, 4:12, :] = choose(odd, outery_ref[...], innery_ref[...])
    odd = lax.axis_index("gx") % 2 == 1
    ext[:, 0:4, :] = choose(odd, innerx_ref[...], outerx_ref[...])
    ext[:, 12:16, :] = choose(odd, outerx_ref[...], innerx_ref[...])
    g = ext[...]
    for _ in range(GSUB):
        center = g[1:-1]
        east = jnp.stack([pltpu.roll(center[i], 15, 0) for i in range(center.shape[0])])
        west = jnp.stack([pltpu.roll(center[i], 1, 0) for i in range(center.shape[0])])
        north = g[2:]
        south = g[:-2]
        step = 0.2 * (east + west + north + south - 4.0 * center) - 0.15 * (east - west) - 0.15 * (north - south)
        g = center + 0.5 * step
    for y in range(TY):
        last = pltpu.roll(g[y], 12, 0)[:TX]
        g4_ref[y] = last
        forcing = (last - own_ref[y]) / (0.5 * GSUB)
        for x in range(TX):
            slot = assign_ref[y, x]
            rows_ref[slot // SLOTS, pl.ds(slot & (SLOTS - 1), 1), :] = forcing[x : x + 1]
            counts_ref[slot] = sub_ref[y, x]
    load.wait()


def split(value):
    high = value.astype(jnp.bfloat16)
    rest = value - high.astype(jnp.float32)
    middle = rest.astype(jnp.bfloat16)
    low = (rest - middle.astype(jnp.float32)).astype(jnp.bfloat16)
    return high, middle, low


def advance_kernel(
    counts,
    mix_ref,
    r0_ref,
    r1_ref,
    r2_ref,
    r3_ref,
    push_ref,
    out_ref,
    tend_ref,
    one,
    two,
    push,
    gather,
    held,
    weights,
    staged,
    sems,
):
    me = lax.axis_index("ha")
    tend_ref[...] = jnp.zeros_like(tend_ref)
    gather[...] = jnp.zeros_like(gather)
    for h in range(FIELDS):
        for g in range(FIELDS):
            weights[h, g] = jnp.full((8, LANES), 0.1 * mix_ref[h, g], jnp.float32)
    lane8 = lax.broadcasted_iota(jnp.int32, (8, LANES), 1)
    half = lane8 & WIDTH
    to_right = half | ((lane8 + 1) & (WIDTH - 1))
    to_left = half | ((lane8 + WIDTH - 1) & (WIDTH - 1))
    slot_row = lax.broadcasted_iota(jnp.int32, (SLOTS, LANES), 0)
    slot_pair = lax.broadcasted_iota(jnp.int32, (SLOTS, LANES), 1) // WIDTH
    arrived = (r0_ref, r1_ref, r2_ref, r3_ref)

    def ends(ref):
        for f in range(FIELDS):
            ref[f, BASE - 1 : BASE, :] = ref[f, BASE : BASE + 1, :]
            ref[f, BASE + LEVELS : BASE + LEVELS + 1, :] = ref[f, BASE + LEVELS - 1 : BASE + LEVELS, :]

    def send(pair, buffer):
        return pltpu.make_async_copy(
            staged.at[buffer], out_ref.at[:, pl.ds(pl.multiple_of(pair * LANES, LANES), LANES)], sems.at[buffer]
        )

    def one_pair(pair, buffer):
        first = me * SLOTS + 2 * pair
        n0 = counts[first]
        n1 = counts[first + 1]
        limit = jnp.where(lane8 < WIDTH, n0, n1)
        steps = jnp.maximum(n0, n1)
        chosen = slot_row == 2 * pair + slot_pair
        spread = jnp.where(chosen, 1.0, 0.0).astype(jnp.bfloat16)
        averaging = jnp.where(chosen, 1.0 / WIDTH, 0.0).astype(jnp.bfloat16)

        for k in range(HELP):
            terms = split(0.1 * push_ref[k])
            total = None
            for term in terms:
                part = lax.dot_general(term, spread, (((0,), (0,)), ((), ())), preferred_element_type=jnp.float32)
                total = part if total is None else total + part
            held[k] = total
            start = (me ^ ORDER[k]) * PART
            for f in range(FIELDS):
                for i in PIECES:
                    push[f, k * PART + i : k * PART + i + 8, :] = held[k, f * PITCH + i : f * PITCH + i + 8, :]
            for f in range(FIELDS):
                for i in PIECES:
                    one[f, pl.ds(BASE + start + i, 8), :] = arrived[k][pl.ds(pair * ROWS + f * PART + i, 8), :]
        ends(one)

        def substep(source, target, index):
            active = index < limit
            for b in range(BLOCKS):
                row = BASE + 8 * b
                here = [source[f, row : row + 8, :] for f in range(FIELDS)]
                warm = [jnp.tanh(s) for s in here]
                for h in range(FIELDS):
                    s = here[h]
                    right = jnp.take_along_axis(s, to_right, axis=1)
                    left = jnp.take_along_axis(s, to_left, axis=1)
                    upper = source[h, row - 1 : row + 7, :]
                    lower = source[h, row + 1 : row + 9, :]
                    mixed = weights[h, 0] * warm[0]
                    for g in range(1, FIELDS):
                        mixed = mixed + weights[h, g] * warm[g]
                    total = 0.7 * s + push[h, 8 * b : 8 * b + 8, :]
                    total = total + 0.1 * (right + left) + 0.05 * (upper + lower)
                    target[h, row : row + 8, :] = jnp.where(active, total + mixed, s)
            ends(target)

        def twice(index, _):
            substep(one, two, 2 * index)
            substep(two, one, 2 * index + 1)
            return 0

        lax.fori_loop(0, steps // 2, twice, 0)

        @pl.when(steps % 2 == 1)
        def _():
            substep(one, two, steps - 1)
            for f in range(FIELDS):
                one[f, BASE : BASE + 64, :] = two[f, BASE : BASE + 64, :]

        for f in range(FIELDS):
            for b in range(BLOCKS):
                n = min(8, LEVELS - 8 * b)
                staged[buffer, pl.ds(8 * b * FIELDS + f, n, stride=FIELDS), :] = one[f, BASE + 8 * b : BASE + 8 * b + n, :]
        send(pair, buffer).start()
        for k in range(HELP):
            owner = me ^ ORDER[k]
            for f in range(FIELDS):
                for i in PIECES:
                    gather[f * PITCH + i : f * PITCH + i + 8, :] = (
                        one[f, pl.ds(BASE + owner * PART + i, 8), :] - arrived[k][pl.ds(pair * ROWS + f * PART + i, 8), :]
                    )
            total = None
            for term in split(gather[...]):
                part = lax.dot_general(averaging, term, (((1,), (1,)), ((), ())), preferred_element_type=jnp.float32)
                total = part if total is None else total + part
            tend_ref[owner] += total

    def each(pair, _):
        one_pair(pair, pair)
        return 0

    lax.fori_loop(0, PAIRS, each, 0)
    for pair in range(PAIRS):
        send(pair, pair).wait()


def placing_kernel(assign_ref, g4_ref, tend_ref, out_ref, rows, turned):
    for x in range(TX):
        for y in range(TY):
            rows[x * TY + y : x * TY + y + 1, :] = g4_ref[y, x : x + 1, :] + tend_ref[pl.ds(assign_ref[y, x], 1), :]
    for f in range(FIELDS):
        turned[f] = pltpu.roll(rows[...], (LANES - f * PITCH) % LANES, 1)
        for x in range(TX):
            out_ref[f, x] = turned[f, x * TY : (x + 1) * TY, :PART]


def swaps(count, first):
    pairs = [(i, (i + 1) % count) for i in range(first, count, 2)]
    return pairs + [(b, a) for a, b in pairs]


def partners(k):
    return [(i, i ^ k) for i in range(HELP)]


def on_device(global_state, crm_state, mixing, substeps, assignment):
    f32 = jnp.float32
    assignment = assignment.T
    substeps = substeps.T
    own = jnp.pad(global_state, ((0, 0), (0, PITCH - PART), (0, 0), (0, 0)))
    own = own.transpose(3, 2, 0, 1).reshape(TY, TX, LANES)
    ny = lax.axis_size("gy")
    nx = lax.axis_size("gx")
    outer = lax.ppermute(own, "gy", swaps(ny, 1))
    inner = lax.ppermute(own, "gy", swaps(ny, 0))

    slotted = pl.pallas_call(
        slotting_kernel,
        out_shape=[jax.ShapeDtypeStruct((PAIRS * ROWS, LANES), f32)] * HELP,
        in_specs=[smem(), pl.BlockSpec(memory_space=pltpu.HBM)],
        out_specs=[vmem()] * HELP,
        scratch_shapes=[
            pltpu.SMEM((COLS,), jnp.int32),
            pltpu.VMEM((TY // 2, ROWS * TX, LANES), f32),
            pltpu.SemaphoreType.DMA((TY // 2,)),
        ],
        compiler_params=pltpu.CompilerParams(vmem_limit_bytes=60 * 1024 * 1024),
    )(assignment, crm_state.reshape(ROWS * TX, TY * WIDTH))
    *slotted, inner, outer = lax.optimization_barrier((*slotted, inner, outer))
    arrived = [lax.ppermute(slotted[k], "ha", partners(ORDER[k])) for k in range(1, HELP)]

    edge = jax.ShapeDtypeStruct((3 * TY, 4, LANES), f32)
    to_outer, to_inner = pl.pallas_call(
        border_kernel,
        out_shape=[edge, edge],
        in_specs=[vmem()] * 3,
        out_specs=[vmem()] * 2,
        scratch_shapes=[pltpu.VMEM((3 * TY, TX, LANES), f32)],
        cost_estimate=pl.CostEstimate(flops=1000, bytes_accessed=300_000, transcendentals=0),
        compiler_params=VM,
    )(own, outer, inner)
    outerx = lax.ppermute(to_outer, "gx", swaps(nx, 1))
    innerx = lax.ppermute(to_inner, "gx", swaps(nx, 0))
    g4, pushes, mine, counts = pl.pallas_call(
        forcing_kernel,
        out_shape=[
            jax.ShapeDtypeStruct((TY, TX, LANES), f32),
            jax.ShapeDtypeStruct((HELP, SLOTS, LANES), f32),
            jax.ShapeDtypeStruct((PAIRS * ROWS, LANES), f32),
            jax.ShapeDtypeStruct((COLS,), jnp.int32),
        ],
        in_specs=[smem(), smem()] + [vmem()] * 5 + [pl.BlockSpec(memory_space=pltpu.HBM)],
        out_specs=[vmem()] * 3 + [smem()],
        scratch_shapes=[pltpu.VMEM((12, 16, LANES), f32), pltpu.SemaphoreType.DMA],
        compiler_params=VM,
    )(assignment, substeps, own, outer, inner, outerx, innerx, slotted[0])
    pushes = lax.all_to_all(pushes, "ha", split_axis=0, concat_axis=0, tiled=True)

    final, tendency = pl.pallas_call(
        advance_kernel,
        out_shape=[
            jax.ShapeDtypeStruct((LEVELS * FIELDS, SLOTS * WIDTH), f32),
            jax.ShapeDtypeStruct((HELP, SLOTS, LANES), f32),
        ],
        in_specs=[smem(), smem()] + [vmem()] * (HELP + 1),
        out_specs=[pl.BlockSpec(memory_space=pltpu.HBM), vmem()],
        scratch_shapes=[
            pltpu.VMEM((FIELDS, SROWS, LANES), f32),
            pltpu.VMEM((FIELDS, SROWS, LANES), f32),
            pltpu.VMEM((FIELDS, 64, LANES), f32),
            pltpu.VMEM((FIELDS * PITCH, LANES), f32),
            pltpu.VMEM((HELP, FIELDS * PITCH, LANES), f32),
            pltpu.VMEM((FIELDS, FIELDS, 8, LANES), f32),
            pltpu.VMEM((PAIRS, LEVELS * FIELDS, LANES), f32),
            pltpu.SemaphoreType.DMA((PAIRS,)),
        ],
        compiler_params=VM,
    )(counts, mixing, mine, *arrived, pushes)
    returned = lax.all_to_all(tendency, "ha", split_axis=0, concat_axis=0, tiled=True)
    placed = pl.pallas_call(
        placing_kernel,
        out_shape=jax.ShapeDtypeStruct((FIELDS, TX, TY, PART), f32),
        in_specs=[smem(), vmem(), vmem()],
        out_specs=vmem(),
        scratch_shapes=[pltpu.VMEM((COLS, LANES), f32), pltpu.VMEM((FIELDS, COLS, LANES), f32)],
        compiler_params=VM,
    )(assignment, g4, returned.reshape(COLS, LANES))
    new_global = placed.transpose(0, 3, 1, 2)
    new_crm = final.reshape(LEVELS, FIELDS, SLOTS * WIDTH).transpose(1, 0, 2)
    return new_global, new_crm


def solution(mesh):
    in_specs = (
        P(None, "ha", "gx", "gy"),
        P(None, "ha", "gx", "gy"),
        P(),
        P("gx", "gy"),
        P("gx", "gy"),
    )
    out_specs = (P(None, "ha", "gx", "gy"), P(None, None, ("gx", "gy", "ha")))
    return jax.shard_map(
        on_device, mesh=mesh, in_specs=in_specs, out_specs=out_specs, check_vma=False
    )
```

```python
import jax
import jax.numpy as jnp
from jax import lax
from jax.experimental import pallas as pl
from jax.experimental.pallas import tpu as pltpu
from jax.sharding import PartitionSpec as P

MAXSUB = 8
GSUB = 4
FIELDS = 8
PART = 15
ROWS = FIELDS * PART
PITCH = 16
LANES = 128
WIDTH = 64
TX = 8
TY = 4
COLS = TX * TY
HELP = 4
ORDER = (0, 2, 1, 3)
SLOTS = 8
PAIRS = SLOTS // 2
LEVELS = PART * HELP
BASE = 8
SROWS = 80
BLOCKS = 8
PIECES = (0, PART - 8)

VM = pltpu.CompilerParams(vmem_limit_bytes=32 * 1024 * 1024)


def smem():
    return pl.BlockSpec(memory_space=pltpu.SMEM)


def vmem():
    return pl.BlockSpec(memory_space=pltpu.VMEM)


def slotting_kernel(assign_ref, crm_ref, s0_ref, s1_ref, s2_ref, s3_ref, inverse, held, sems):
    me = lax.axis_index("ha")
    loads = [
        pltpu.make_async_copy(crm_ref.at[:, i * LANES : (i + 1) * LANES], held.at[i], sems.at[i]) for i in range(TY // 2)
    ]
    for load in loads:
        load.start()
    for x in range(TX):
        for y in range(TY):
            inverse[assign_ref[y, x]] = x * TY + y
    lane = lax.broadcasted_iota(jnp.int32, (ROWS, LANES), 1)

    low = jnp.where(lane < WIDTH, 1, 0)

    def column(slot):
        place = inverse[slot]
        y = place % TY
        return held[y // 2, pl.ds(place // TY, ROWS, stride=TX), :], y % 2

    def both(slot):
        first, at = column(slot)
        second, to = column(slot + 1)
        same = jnp.where(at == to, 1, 0)
        other = low ^ at
        turned = jnp.where(same == 1, at, other) == 1
        kept = other + same == 2
        moved = pltpu.roll(jnp.where(turned, first, second), jnp.where(same == 1, WIDTH, at * WIDTH), 1)
        return jnp.where(kept, jnp.where(at == 1, second, first), moved)

    for load in loads:
        load.wait()
    for k, part in enumerate((s0_ref, s1_ref, s2_ref, s3_ref)):
        for pair in range(PAIRS):
            slot = (me ^ ORDER[k]) * SLOTS + 2 * pair
            part[pair * ROWS : (pair + 1) * ROWS, :] = both(slot)


def choose(odd, first, second):
    return jnp.where(odd, first, second)


def border_kernel(own_ref, outer_ref, inner_ref, to_outer_ref, to_inner_ref, tall):
    odd = lax.axis_index("gy") % 2 == 1
    tall[0:4] = choose(odd, inner_ref[...], outer_ref[...])
    tall[4:8] = own_ref[...]
    tall[8:12] = choose(odd, outer_ref[...], inner_ref[...])
    odd = lax.axis_index("gx") % 2 == 1
    low, high = tall[:, 0:4, :], tall[:, TX - 4 : TX, :]
    to_outer_ref[...] = choose(odd, high, low)
    to_inner_ref[...] = choose(odd, low, high)


def forcing_kernel(assign_ref, sub_ref, own_ref, outery_ref, innery_ref, outerx_ref, innerx_ref, s0_ref, g4_ref, rows_ref, mine_ref, counts_ref, ext, sem):
    load = pltpu.make_async_copy(s0_ref, mine_ref, sem)
    load.start()
    odd = lax.axis_index("gy") % 2 == 1
    ext[0:4, 4:12, :] = choose(odd, innery_ref[...], outery_ref[...])
    ext[4:8, 4:12, :] = own_ref[...]
    ext[8:12, 4:12, :] = choose(odd, outery_ref[...], innery_ref[...])
    odd = lax.axis_index("gx") % 2 == 1
    ext[:, 0:4, :] = choose(odd, innerx_ref[...], outerx_ref[...])
    ext[:, 12:16, :] = choose(odd, outerx_ref[...], innerx_ref[...])
    g = ext[...]
    for _ in range(GSUB):
        center = g[1:-1]
        east = jnp.stack([pltpu.roll(center[i], 15, 0) for i in range(center.shape[0])])
        west = jnp.stack([pltpu.roll(center[i], 1, 0) for i in range(center.shape[0])])
        north = g[2:]
        south = g[:-2]
        step = 0.2 * (east + west + north + south - 4.0 * center) - 0.15 * (east - west) - 0.15 * (north - south)
        g = center + 0.5 * step
    for y in range(TY):
        last = pltpu.roll(g[y], 12, 0)[:TX]
        g4_ref[y] = last
        forcing = (last - own_ref[y]) / (0.5 * GSUB)
        for x in range(TX):
            slot = assign_ref[y, x]
            rows_ref[slot // SLOTS, pl.ds(slot & (SLOTS - 1), 1), :] = forcing[x : x + 1]
            counts_ref[slot] = sub_ref[y, x]
    load.wait()


def split(value):
    high = value.astype(jnp.bfloat16)
    rest = value - high.astype(jnp.float32)
    middle = rest.astype(jnp.bfloat16)
    low = (rest - middle.astype(jnp.float32)).astype(jnp.bfloat16)
    return high, middle, low


def advance_kernel(
    counts,
    mix_ref,
    r0_ref,
    r1_ref,
    r2_ref,
    r3_ref,
    push_ref,
    out_ref,
    tend_ref,
    one,
    two,
    push,
    gather,
    held,
    weights,
    staged,
    sems,
):
    me = lax.axis_index("ha")
    tend_ref[...] = jnp.zeros_like(tend_ref)
    gather[...] = jnp.zeros_like(gather)
    for h in range(FIELDS):
        for g in range(FIELDS):
            weights[h, g] = jnp.full((8, LANES), 0.1 * mix_ref[h, g], jnp.float32)
    lane8 = lax.broadcasted_iota(jnp.int32, (8, LANES), 1)
    half = lane8 & WIDTH
    to_right = half | ((lane8 + 1) & (WIDTH - 1))
    to_left = half | ((lane8 + WIDTH - 1) & (WIDTH - 1))
    slot_row = lax.broadcasted_iota(jnp.int32, (SLOTS, LANES), 0)
    slot_pair = lax.broadcasted_iota(jnp.int32, (SLOTS, LANES), 1) // WIDTH
    arrived = (r0_ref, r1_ref, r2_ref, r3_ref)

    def ends(ref):
        for f in range(FIELDS):
            ref[f, BASE - 1 : BASE, :] = ref[f, BASE : BASE + 1, :]
            ref[f, BASE + LEVELS : BASE + LEVELS + 1, :] = ref[f, BASE + LEVELS - 1 : BASE + LEVELS, :]

    def send(pair, buffer):
        return pltpu.make_async_copy(
            staged.at[buffer], out_ref.at[:, pl.ds(pl.multiple_of(pair * LANES, LANES), LANES)], sems.at[buffer]
        )

    def one_pair(pair, buffer):
        first = me * SLOTS + 2 * pair
        n0 = counts[first]
        n1 = counts[first + 1]
        limit = jnp.where(lane8 < WIDTH, n0, n1)
        steps = jnp.maximum(n0, n1)
        chosen = slot_row == 2 * pair + slot_pair
        spread = jnp.where(chosen, 1.0, 0.0).astype(jnp.bfloat16)
        averaging = jnp.where(chosen, 1.0 / WIDTH, 0.0).astype(jnp.bfloat16)

        for k in range(HELP):
            terms = split(0.1 * push_ref[k])
            total = None
            for term in terms:
                part = lax.dot_general(term, spread, (((0,), (0,)), ((), ())), preferred_element_type=jnp.float32)
                total = part if total is None else total + part
            held[k] = total
            start = (me ^ ORDER[k]) * PART
            for f in range(FIELDS):
                for i in PIECES:
                    push[f, k * PART + i : k * PART + i + 8, :] = held[k, f * PITCH + i : f * PITCH + i + 8, :]
            for f in range(FIELDS):
                for i in PIECES:
                    one[f, pl.ds(BASE + start + i, 8), :] = arrived[k][pl.ds(pair * ROWS + f * PART + i, 8), :]
        ends(one)

        def substep(source, target, index):
            active = index < limit
            for b in range(BLOCKS):
                row = BASE + 8 * b
                here = [source[f, row : row + 8, :] for f in range(FIELDS)]
                warm = [jnp.tanh(s) for s in here]
                for h in range(FIELDS):
                    s = here[h]
                    right = jnp.take_along_axis(s, to_right, axis=1)
                    left = jnp.take_along_axis(s, to_left, axis=1)
                    upper = source[h, row - 1 : row + 7, :]
                    lower = source[h, row + 1 : row + 9, :]
                    mixed = weights[h, 0] * warm[0]
                    for g in range(1, FIELDS):
                        mixed = mixed + weights[h, g] * warm[g]
                    total = 0.7 * s + push[h, 8 * b : 8 * b + 8, :]
                    total = total + 0.1 * (right + left) + 0.05 * (upper + lower)
                    target[h, row : row + 8, :] = jnp.where(active, total + mixed, s)
            ends(target)

        def twice(index, _):
            substep(one, two, 2 * index)
            substep(two, one, 2 * index + 1)
            return 0

        lax.fori_loop(0, steps // 2, twice, 0)

        @pl.when(steps % 2 == 1)
        def _():
            substep(one, two, steps - 1)
            for f in range(FIELDS):
                one[f, BASE : BASE + 64, :] = two[f, BASE : BASE + 64, :]

        for f in range(FIELDS):
            for b in range(BLOCKS):
                n = min(8, LEVELS - 8 * b)
                staged[buffer, pl.ds(8 * b * FIELDS + f, n, stride=FIELDS), :] = one[f, BASE + 8 * b : BASE + 8 * b + n, :]
        send(pair, buffer).start()
        for k in range(HELP):
            owner = me ^ ORDER[k]
            for f in range(FIELDS):
                for i in PIECES:
                    gather[f * PITCH + i : f * PITCH + i + 8, :] = (
                        one[f, pl.ds(BASE + owner * PART + i, 8), :] - arrived[k][pl.ds(pair * ROWS + f * PART + i, 8), :]
                    )
            total = None
            for term in split(gather[...]):
                part = lax.dot_general(averaging, term, (((1,), (1,)), ((), ())), preferred_element_type=jnp.float32)
                total = part if total is None else total + part
            tend_ref[owner] += total

    def each(pair, _):
        one_pair(pair, pair)
        return 0

    lax.fori_loop(0, PAIRS, each, 0)
    for pair in range(PAIRS):
        send(pair, pair).wait()


def placing_kernel(assign_ref, g4_ref, tend_ref, out_ref, rows, turned):
    for x in range(TX):
        for y in range(TY):
            rows[x * TY + y : x * TY + y + 1, :] = g4_ref[y, x : x + 1, :] + tend_ref[pl.ds(assign_ref[y, x], 1), :]
    for f in range(FIELDS):
        turned[f] = pltpu.roll(rows[...], (LANES - f * PITCH) % LANES, 1)
        for x in range(TX):
            out_ref[f, x] = turned[f, x * TY : (x + 1) * TY, :PART]


def swaps(count, first):
    pairs = [(i, (i + 1) % count) for i in range(first, count, 2)]
    return pairs + [(b, a) for a, b in pairs]


def partners(k):
    return [(i, i ^ k) for i in range(HELP)]


def on_device(global_state, crm_state, mixing, substeps, assignment):
    f32 = jnp.float32
    assignment = assignment.T
    substeps = substeps.T
    own = jnp.pad(global_state, ((0, 0), (0, PITCH - PART), (0, 0), (0, 0)))
    own = own.transpose(3, 2, 0, 1).reshape(TY, TX, LANES)
    ny = lax.axis_size("gy")
    nx = lax.axis_size("gx")
    outer = lax.ppermute(own, "gy", swaps(ny, 1))
    inner = lax.ppermute(own, "gy", swaps(ny, 0))

    slotted = pl.pallas_call(
        slotting_kernel,
        out_shape=[jax.ShapeDtypeStruct((PAIRS * ROWS, LANES), f32)] * HELP,
        in_specs=[smem(), pl.BlockSpec(memory_space=pltpu.HBM)],
        out_specs=[vmem()] * HELP,
        scratch_shapes=[
            pltpu.SMEM((COLS,), jnp.int32),
            pltpu.VMEM((TY // 2, ROWS * TX, LANES), f32),
            pltpu.SemaphoreType.DMA((TY // 2,)),
        ],
        compiler_params=pltpu.CompilerParams(vmem_limit_bytes=60 * 1024 * 1024),
    )(assignment, crm_state.reshape(ROWS * TX, TY * WIDTH))
    *slotted, inner, outer = lax.optimization_barrier((*slotted, inner, outer))
    arrived = [lax.ppermute(slotted[k], "ha", partners(ORDER[k])) for k in range(1, HELP)]

    edge = jax.ShapeDtypeStruct((3 * TY, 4, LANES), f32)
    to_outer, to_inner = pl.pallas_call(
        border_kernel,
        out_shape=[edge, edge],
        in_specs=[vmem()] * 3,
        out_specs=[vmem()] * 2,
        scratch_shapes=[pltpu.VMEM((3 * TY, TX, LANES), f32)],
        cost_estimate=pl.CostEstimate(flops=1000, bytes_accessed=300_000, transcendentals=0),
        compiler_params=VM,
    )(own, outer, inner)
    outerx = lax.ppermute(to_outer, "gx", swaps(nx, 1))
    innerx = lax.ppermute(to_inner, "gx", swaps(nx, 0))
    g4, pushes, mine, counts = pl.pallas_call(
        forcing_kernel,
        out_shape=[
            jax.ShapeDtypeStruct((TY, TX, LANES), f32),
            jax.ShapeDtypeStruct((HELP, SLOTS, LANES), f32),
            jax.ShapeDtypeStruct((PAIRS * ROWS, LANES), f32),
            jax.ShapeDtypeStruct((COLS,), jnp.int32),
        ],
        in_specs=[smem(), smem()] + [vmem()] * 5 + [pl.BlockSpec(memory_space=pltpu.HBM)],
        out_specs=[vmem()] * 3 + [smem()],
        scratch_shapes=[pltpu.VMEM((12, 16, LANES), f32), pltpu.SemaphoreType.DMA],
        compiler_params=VM,
    )(assignment, substeps, own, outer, inner, outerx, innerx, slotted[0])
    pushes = lax.all_to_all(pushes, "ha", split_axis=0, concat_axis=0, tiled=True)

    final, tendency = pl.pallas_call(
        advance_kernel,
        out_shape=[
            jax.ShapeDtypeStruct((LEVELS * FIELDS, SLOTS * WIDTH), f32),
            jax.ShapeDtypeStruct((HELP, SLOTS, LANES), f32),
        ],
        in_specs=[smem(), smem()] + [vmem()] * (HELP + 1),
        out_specs=[pl.BlockSpec(memory_space=pltpu.HBM), vmem()],
        scratch_shapes=[
            pltpu.VMEM((FIELDS, SROWS, LANES), f32),
            pltpu.VMEM((FIELDS, SROWS, LANES), f32),
            pltpu.VMEM((FIELDS, 64, LANES), f32),
            pltpu.VMEM((FIELDS * PITCH, LANES), f32),
            pltpu.VMEM((HELP, FIELDS * PITCH, LANES), f32),
            pltpu.VMEM((FIELDS, FIELDS, 8, LANES), f32),
            pltpu.VMEM((PAIRS, LEVELS * FIELDS, LANES), f32),
            pltpu.SemaphoreType.DMA((PAIRS,)),
        ],
        compiler_params=VM,
    )(counts, mixing, mine, *arrived, pushes)
    returned = lax.all_to_all(tendency, "ha", split_axis=0, concat_axis=0, tiled=True)
    placed = pl.pallas_call(
        placing_kernel,
        out_shape=jax.ShapeDtypeStruct((FIELDS, TX, TY, PART), f32),
        in_specs=[smem(), vmem(), vmem()],
        out_specs=vmem(),
        scratch_shapes=[pltpu.VMEM((COLS, LANES), f32), pltpu.VMEM((FIELDS, COLS, LANES), f32)],
        compiler_params=VM,
    )(assignment, g4, returned.reshape(COLS, LANES))
    new_global = placed.transpose(0, 3, 1, 2)
    new_crm = final.reshape(LEVELS, FIELDS, SLOTS * WIDTH).transpose(1, 0, 2)
    return new_global, new_crm


def solution(mesh):
    in_specs = (
        P(None, "ha", "gx", "gy"),
        P(None, "ha", "gx", "gy"),
        P(),
        P("gx", "gy"),
        P("gx", "gy"),
    )
    out_specs = (P(None, "ha", "gx", "gy"), P(None, None, ("gx", "gy", "ha")))
    return jax.shard_map(
        on_device, mesh=mesh, in_specs=in_specs, out_specs=out_specs, check_vma=False
    )
```
